256 devices in a mesh: dp: 32 (over z, y_hi, core), fsdp: 8 (over y_lo, x).
Axes of the slice: x: 4, y: 4 (y_hi: 2, y_lo: 2; y = y_hi * 2 + y_lo), z: 8, core: 2. Of those that a mesh axis runs over, the one named last changes fastest.
Arguments:
- query_embedding_rows: bfloat16 [2048, 2048], P('dp', 'fsdp'), may hold values from -6 to 6
- passage_embedding_rows: bfloat16 [2048, 2048], P('dp', 'fsdp'), may hold values from -6 to 6
- positive: int32 [2048], P('dp'), may hold values from 0 to 2047
- layer_input_rows: bfloat16 [512, 128, 4096], P(('dp', 'fsdp')), may hold values from -6 to 6
- input_norm_gain: float32 [4096], replicated, may hold values from 0.25 to 2.75
- frozen_projection_weight: bfloat16 [4096, 3072], P('fsdp'), may hold values from -0.09375 to 0.09375
- adapter_down_maps: bfloat16 [4096, 48], P('fsdp'), may hold values from -0.09375 to 0.09375
- adapter_up_maps: bfloat16 [3072, 16], P('fsdp'), may hold values from -1.5 to 1.5
Outputs:
- query_grad: float32 [2048, 2048], P('dp', 'fsdp')
- passage_gradient: float32 [2048, 2048], P('dp', 'fsdp')
- grad_down: float32 [4096, 48], P('fsdp')
- grad_up: float32 [3072, 16], P('fsdp')
The draws below stay inside these ranges and needn't reach their ends.
All inputs are finite; a program needn't handle non-finite values.
Results may differ from the reference program's by a relative error of at most 0.007.
The reference program's roundings to bfloat16 on the way count: a program that leaves them out, or rounds other values in their place, can miss the bound.
Values may be sent and summed in bfloat16 or wider, within the bound.
No kernel may reach another device: no remote copies, remote signals or barrier semaphores. Data moves between devices by JAX's collectives and lax.ppermute only.
A program may use at most 128 MiB of HBM per device.

```python
import math
import jax
import jax.numpy as jnp
from jax import lax

MODEL_WIDTH = 4096
HD = 128
HQ = 16
HK = 4
ADAPTER_RANK = 16
L = 128
SEQ_DEV = 2
PAIR_DP = 64
EMB = 2048
QUERY_KEY_VALUE = 3072
NPAIR = 2048
NSEQ = 512
N_DP = 32
N_FSDP = 8
DEVICES = 256


def draw_input_norm_gain(key, part):
    key = jax.random.fold_in(key, 11)
    place = jnp.arange(MODEL_WIDTH, dtype=jnp.float32) / (MODEL_WIDTH - 1)
    base = 0.5 + place
    rough = jnp.exp(jax.random.uniform(key, (MODEL_WIDTH,), jnp.float32, -0.3, 0.3))
    return (base * rough).astype(jnp.float32)


def with_ends(array, stream_key, smallest, top_value):
    index_at = [jax.random.randint(jax.random.fold_in(stream_key, axis), (), 0, length) for axis, length in enumerate(array.shape)]
    longest = array.shape.index(max(array.shape))
    next_to = index_at[:longest] + [(index_at[longest] + 1) % array.shape[longest]] + index_at[longest + 1:]
    return array.at[tuple(index_at)].set(smallest).at[tuple(next_to)].set(top_value)


def shard_levels(own_key, shape, split, smallest, high):
    def one(axis_at, parts):
        heights = jax.random.uniform(jax.random.fold_in(jax.random.fold_in(own_key, 6), axis_at), (parts,), jnp.float32, smallest / len(split), high / len(split))
        return jnp.repeat(jnp.exp(heights), shape[axis_at] // parts).reshape((-1,) + (1,) * (len(shape) - axis_at - 1))

    factor_of = one(*split[0])
    for cut in split[1:]:
        factor_of = factor_of * one(*cut)
    return factor_of


def noise(own_key, dims, spread, bound, cuts=(), kind=jnp.bfloat16):
    entries = jax.random.normal(own_key, dims, jnp.float32) * spread
    if len(cuts) > 0:
        entries = shard_levels(own_key, dims, cuts, -0.22, 0.18) * entries
    return jnp.clip(entries, min=-bound, max=bound).astype(kind)


def setup_inputs(seed: int = 0) -> dict:
    key_list = jax.random.split(jax.random.key(seed), 9)
    query_embedding_rows = noise(key_list[0], (NPAIR, EMB), 1.0, 6.0, ((0, 32), (1, 8)))
    passage_embedding_rows = noise(key_list[1], (NPAIR, EMB), 1.0, 6.0, ((0, 32), (1, 8)))
    positive = with_ends(jax.random.randint(key_list[2], (NPAIR,), 0, NPAIR), jax.random.fold_in(key_list[2], 1), 0, NPAIR - 1).astype(jnp.int32)
    layer_input_rows = noise(key_list[3], (NSEQ, L, MODEL_WIDTH), 1.0, 6.0, ((0, 256),))
    input_norm_gain = draw_input_norm_gain(jax.random.fold_in(key_list[8], 71), 0)
    frozen_projection_weight = noise(key_list[5], (MODEL_WIDTH, QUERY_KEY_VALUE), MODEL_WIDTH ** -0.5, 0.09375, ((0, 8),))
    adapter_down_maps = noise(key_list[6], (MODEL_WIDTH, 3 * ADAPTER_RANK), MODEL_WIDTH ** -0.5, 0.09375, ((0, 8),))
    adapter_up_maps = noise(key_list[7], (QUERY_KEY_VALUE, ADAPTER_RANK), ADAPTER_RANK ** -0.5, 1.5, ((0, 8),))
    return dict(query_embedding_rows=query_embedding_rows, passage_embedding_rows=passage_embedding_rows, positive=positive, layer_input_rows=layer_input_rows, input_norm_gain=input_norm_gain, frozen_projection_weight=frozen_projection_weight, adapter_down_maps=adapter_down_maps, adapter_up_maps=adapter_up_maps)


EPS_NORM = 1e-06
SOFTMAX_TEMPER = 0.02
ADAPTER_SCALE = 2.0
RMS_EPS = 1e-05
ROPE_BASE = 10000.0
MAX_NORM = 1.0
PRECISE = lax.Precision.HIGHEST

def rounded(value):
    return lax.optimization_barrier(value.astype(jnp.bfloat16)).astype(jnp.float32)

def through(value):
    return value + lax.stop_gradient(rounded(value) - value)

def normalize_rows(token_rows, gain):
    values = token_rows.astype(jnp.float32)
    scale = lax.rsqrt(lax.optimization_barrier(jnp.mean(values * values, axis=-1, keepdims=True)) + RMS_EPS)
    return (values * scale * gain[None, :]).astype(jnp.bfloat16)

def rotate_pairs(values):
    half_size = HD // 2
    freqs = ROPE_BASE ** (-(jnp.arange(half_size, dtype=jnp.float32) * 2.0) / HD)
    angles = jnp.arange(L, dtype=jnp.float32)[:, None] * freqs[None, :]
    cosine = jnp.cos(angles)[None, :, None, :]
    sine = jnp.sin(angles)[None, :, None, :]
    first = values[..., :half_size]
    second = values[..., half_size:]
    return jnp.concatenate([first * cosine - second * sine, second * cosine + first * sine], axis=-1)

def attend(queries, keys, values):
    seq_count = queries.shape[0]
    grouped = queries.reshape(seq_count, L, HK, HQ // HK, HD)
    similarity_scores = jnp.einsum('slkgd,smkd->skglm', grouped, keys, precision=PRECISE) / math.sqrt(HD)
    causal = jnp.arange(L)[:, None] >= jnp.arange(L)[None, :]
    similarity_scores = jnp.where(causal, similarity_scores, -1e+30)
    row_max = lax.stop_gradient(lax.optimization_barrier(jnp.max(similarity_scores, axis=-1, keepdims=True)))
    weights = jnp.exp(similarity_scores - row_max)
    weights = through(weights / lax.optimization_barrier(jnp.sum(weights, axis=-1, keepdims=True)))
    outputs = jnp.einsum('skglm,smkd->slkgd', weights, values, precision=PRECISE)
    return lax.optimization_barrier(jnp.mean(outputs.reshape(seq_count, L, HQ * HD), axis=1))

def surrogate(low_rank_activation, up_map_transposed, frozen_projection, embedding_gradient_pair):
    seq_count = embedding_gradient_pair.shape[0]
    low_rank = through(low_rank_activation)
    slice_list = []
    offset = 0
    for block, span_width in enumerate((HQ * HD, HK * HD, HK * HD)):
        slice_list.append(jnp.dot(low_rank[:, ADAPTER_RANK * block:ADAPTER_RANK * (block + 1)], up_map_transposed[offset:offset + span_width].T, precision=PRECISE))
        offset = offset + span_width
    projection_output = frozen_projection + ADAPTER_SCALE * jnp.concatenate(slice_list, axis=1)
    queries = projection_output[:, :HQ * HD].reshape(seq_count, L, HQ, HD)
    keys = projection_output[:, HQ * HD:(HQ + HK) * HD].reshape(seq_count, L, HK, HD)
    values = projection_output[:, (HQ + HK) * HD:].reshape(seq_count, L, HK, HD)
    queries = through(rotate_pairs(queries))
    keys = through(rotate_pairs(keys))
    values = through(values)
    embedded = attend(queries, keys, values)
    return jnp.sum(embedded * embedding_gradient_pair)

def adapter_gradient_pair(normalized_input, frozen_projection, low_rank_activation, adapter_up_maps, embedding_gradient_pair):
    up_map_transposed = adapter_up_maps.astype(jnp.float32)
    _, pullback = jax.vjp(lambda low_in, up_in: surrogate(low_in, up_in, frozen_projection, embedding_gradient_pair), low_rank_activation, up_map_transposed)
    dlow, up_map_gradient = pullback(jnp.ones((), jnp.float32))
    down_map_gradient = jnp.dot(normalized_input.astype(jnp.float32).T, dlow, precision=PRECISE)
    return (down_map_gradient, up_map_gradient)

def reference(query_embedding_rows, passage_embedding_rows, positive, layer_input_rows, input_norm_gain, frozen_projection_weight, adapter_down_maps, adapter_up_maps):
    query_f32 = query_embedding_rows.astype(jnp.float32)
    passage_single_float = passage_embedding_rows.astype(jnp.float32)
    query_norm_value = jnp.sqrt(lax.optimization_barrier(jnp.sum(query_f32 * query_f32, axis=1)) + EPS_NORM)
    passage_norm_value = jnp.sqrt(lax.optimization_barrier(jnp.sum(passage_single_float * passage_single_float, axis=1)) + EPS_NORM)
    unscaled_scores = jnp.dot(query_embedding_rows, passage_embedding_rows.T, preferred_element_type=jnp.float32)
    similarity_scores = unscaled_scores / (query_norm_value[:, None] * passage_norm_value[None, :] * SOFTMAX_TEMPER)
    row_max = lax.optimization_barrier(jnp.max(similarity_scores, axis=1, keepdims=True))
    expd = jnp.exp(similarity_scores - row_max)
    softmax = expd / lax.optimization_barrier(jnp.sum(expd, axis=1, keepdims=True))
    onehot = (jnp.arange(NPAIR, dtype=jnp.int32)[None, :] == positive[:, None]).astype(jnp.float32)
    score_gradient = softmax - onehot
    cross_term = lax.optimization_barrier(jnp.sum(score_gradient * similarity_scores, axis=1))
    column_loss_term = lax.optimization_barrier(jnp.sum(score_gradient * similarity_scores, axis=0))
    weighted_passages = score_gradient / (passage_norm_value[None, :] * SOFTMAX_TEMPER)
    query_grad = jnp.dot(weighted_passages, passage_single_float, precision=PRECISE) / query_norm_value[:, None] - (cross_term / (query_norm_value * query_norm_value))[:, None] * query_f32
    pulled_gradient = jnp.dot(score_gradient.T, query_f32 / query_norm_value[:, None], precision=PRECISE)
    passage_gradient = pulled_gradient / (passage_norm_value * SOFTMAX_TEMPER)[:, None] - (column_loss_term / (passage_norm_value * passage_norm_value))[:, None] * passage_single_float
    rerun = query_grad.reshape(N_DP, PAIR_DP, EMB)[:, :N_FSDP * SEQ_DEV].reshape(DEVICES, SEQ_DEV, EMB)
    blocks = layer_input_rows.reshape(DEVICES, SEQ_DEV * L, MODEL_WIDTH)

    def block_step(totals, block_items):
        token_rows, embedding_gradient_pair = block_items
        normalized_input = normalize_rows(token_rows, input_norm_gain)
        frozen_projection = jnp.dot(normalized_input, frozen_projection_weight, preferred_element_type=jnp.float32)
        low_rank_activation = jnp.dot(normalized_input, adapter_down_maps, preferred_element_type=jnp.float32)
        down_map_gradient, up_map_gradient = adapter_gradient_pair(normalized_input, frozen_projection, low_rank_activation, adapter_up_maps, embedding_gradient_pair)
        return ((totals[0] + down_map_gradient, totals[1] + up_map_gradient), None)
    start_totals = (jnp.zeros((MODEL_WIDTH, 3 * ADAPTER_RANK), jnp.float32), jnp.zeros((QUERY_KEY_VALUE, ADAPTER_RANK), jnp.float32))
    (down_total, up_total), _ = lax.scan(block_step, start_totals, (blocks, rerun))
    grad_norm = jnp.sqrt(jnp.sum(down_total * down_total) + jnp.sum(up_total * up_total))
    clip_factor = jnp.minimum(1.0, MAX_NORM / (grad_norm + 1e-06))
    unit_scale = math.sqrt(3 * MODEL_WIDTH * ADAPTER_RANK + QUERY_KEY_VALUE * ADAPTER_RANK)
    return (query_grad, passage_gradient, down_total * (clip_factor * unit_scale), up_total * (clip_factor * unit_scale))
```

```python
import functools
import math

import jax
import jax.numpy as jnp
import numpy as np
from jax import lax
from jax.experimental import pallas as pl
from jax.experimental.pallas import tpu as pltpu
from jax.sharding import PartitionSpec as P

MODEL_WIDTH = 4096
HD = 128
HQ = 16
HK = 4
GROUP = HQ // HK
ADAPTER_RANK = 16
L = 128
EPS_NORM = 1e-06
SOFTMAX_TEMPER = 0.02
ADAPTER_SCALE = 2.0
RMS_EPS = 1e-05
ROPE_BASE = 10000.0
MAX_NORM = 1.0

N_DP = 32
N_FSDP = 8
RING = N_DP // 2
ROWS = MODEL_WIDTH // N_FSDP
UP_ROWS = (HQ + 2 * HK) * HD // N_FSDP
COLS = (GROUP + 2) * HD
PACK = 3 * ADAPTER_RANK + ADAPTER_RANK
LOW = 3 * ADAPTER_RANK
F32 = jnp.float32
BF16 = jnp.bfloat16
VMEM_LIMIT = 48 * 1024 * 1024

NN = (((1,), (0,)), ((), ()))
NT = (((1,), (1,)), ((), ()))
TN = (((0,), (0,)), ((), ()))


def dot(a, b, dims=NN):
    return lax.dot_general(a, b, dims, preferred_element_type=F32)


def split(x):
    head = x.astype(BF16)
    return head, (x - head.astype(F32)).astype(BF16)


def params():
    return pltpu.CompilerParams(vmem_limit_bytes=VMEM_LIMIT)


def cost(flops, bytes_accessed):
    return pl.CostEstimate(flops=int(flops), bytes_accessed=int(bytes_accessed), transcendentals=0)


VMEM = pl.BlockSpec(memory_space=pltpu.VMEM)
SMEM = pl.BlockSpec(memory_space=pltpu.SMEM)
ANY = pl.BlockSpec(memory_space=pl.ANY)


def rope_tables():
    half = HD // 2
    freqs = np.power(
        np.float32(ROPE_BASE), -(np.arange(half, dtype=np.float32) * np.float32(2.0)) / np.float32(HD)
    ).astype(np.float32)
    angles = np.arange(L, dtype=np.float32)[:, None] * freqs[None, :]
    cosine = np.cos(angles).astype(np.float32)
    sine = np.sin(angles).astype(np.float32)
    return np.concatenate([cosine, cosine], 1), np.concatenate([-sine, sine], 1)


def normalize_kernel(x_ref, gain_ref, first_ref, second_ref):
    for s, out_ref in enumerate((first_ref, second_ref)):
        values = x_ref[s].astype(F32)
        scale = lax.rsqrt(jnp.mean(values * values, axis=-1, keepdims=True) + RMS_EPS)
        out_ref[...] = (values * scale * gain_ref[...]).astype(BF16)


def normalize(x, gain):
    shape = jax.ShapeDtypeStruct((L, MODEL_WIDTH), BF16)
    step = 32
    return pl.pallas_call(
        normalize_kernel,
        name="normalize",
        grid=(L // step,),
        in_specs=[
            pl.BlockSpec((2, step, MODEL_WIDTH), lambda i: (0, i, 0)),
            pl.BlockSpec((1, MODEL_WIDTH), lambda i: (0, 0)),
        ],
        out_specs=[pl.BlockSpec((step, MODEL_WIDTH), lambda i: (i, 0))] * 2,
        out_shape=[shape, shape],
        compiler_params=params(),
        cost_estimate=cost(6 * 2 * L * MODEL_WIDTH, 8 * L * MODEL_WIDTH),
    )(x, gain.reshape(1, MODEL_WIDTH))


def eye_mask(n, m):
    return lax.broadcasted_iota(jnp.int32, (n, m), 0) == lax.broadcasted_iota(jnp.int32, (n, m), 1)


def column_of(row, n):
    return jnp.sum(jnp.where(eye_mask(n, row.shape[1]), row, 0.0), axis=1, keepdims=True)


def chunk_of(c, own_ref, other_ref, size=256):
    per = own_ref.shape[0] // size
    ref = own_ref if c < per else other_ref
    return ref[(c % per) * size : (c % per + 1) * size, :]


def partial_scores_kernel(q_ref, own_ref, other_ref, out_ref):
    q = q_ref[...]
    ones = jnp.ones((16, 256), BF16)
    rows = lax.broadcasted_iota(jnp.int32, (8, 256), 0)

    def square_row(block):
        values = block.astype(F32)
        head, rest = split(values * values)
        return (dot(ones, head, NT) + dot(ones, rest, NT))[0:8]

    q_row = square_row(jnp.concatenate([q, jnp.zeros((256 - 64, 256), BF16)], axis=0))
    for c in range(N_FSDP):
        passages = chunk_of(c, own_ref, other_ref)
        out_ref[c, 0:64, :] = dot(q, passages, NT)
        out_ref[c, 64:72, :] = jnp.where(
            rows == 0, square_row(passages), jnp.where(rows == 1, q_row, 0.0)
        )


def finish_scores_kernel(parts_ref, out_ref):
    total = parts_ref[0]
    for c in range(1, N_FSDP):
        total = total + parts_ref[c]
    p_norm = jnp.sqrt(total[64:65] + EPS_NORM)
    q_norm_row = jnp.sqrt(total[65:66] + EPS_NORM)
    q_norm = column_of(q_norm_row, 64)
    scores = total[0:64] / (q_norm * p_norm * SOFTMAX_TEMPER)
    rows = lax.broadcasted_iota(jnp.int32, (8, 256), 0)
    tail = jnp.where(rows == 0, p_norm, jnp.where(rows == 1, q_norm_row, 0.0))
    for c in range(N_FSDP):
        out_ref[c, 0:64, :] = scores
        out_ref[c, 64:72, :] = tail


def query_grad_kernel(s_ref, q_ref, pos_ref, own_ref, other_ref, grad_ref, w_ref, col_ref):
    top = jnp.max(s_ref[0, 0:64, :], axis=1, keepdims=True)
    for c in range(1, N_FSDP):
        top = jnp.maximum(top, jnp.max(s_ref[c, 0:64, :], axis=1, keepdims=True))
    norm = jnp.zeros((64, 1), F32)
    for c in range(N_FSDP):
        norm = norm + jnp.sum(jnp.exp(s_ref[c, 0:64, :] - top), axis=1, keepdims=True)
    q_norm = column_of(s_ref[0, 65:66, :], 64)
    place = pos_ref[...]
    lane = lax.broadcasted_iota(jnp.int32, (64, 256), 1)
    cross = jnp.zeros((64, 1), F32)
    total = jnp.zeros((64, 256), F32)
    for c in range(N_FSDP):
        s = s_ref[c, 0:64, :]
        p_norm = s_ref[c, 64:65, :]
        grad = jnp.exp(s - top) / norm - jnp.where(lane + 256 * c == place, 1.0, 0.0)
        terms = grad * s
        cross = cross + jnp.sum(terms, axis=1, keepdims=True)
        column = jnp.sum(terms, axis=0, keepdims=True)
        col_ref[c] = jnp.broadcast_to(column / (p_norm * p_norm), (8, 256))
        weight = grad / (p_norm * SOFTMAX_TEMPER)
        w_ref[c] = weight / q_norm
        head, rest = split(weight)
        both = dot(jnp.concatenate([head, rest], axis=0), chunk_of(c, own_ref, other_ref))
        total = total + both[0:64] + both[64:128]
    grad_ref[...] = total / q_norm - (cross / (q_norm * q_norm)) * q_ref[...].astype(F32)


def passage_terms_kernel(w_ref, col_ref, q_ref, own_ref, other_ref, keep_ref, give_ref):
    q = q_ref[...]
    twice = jnp.concatenate([q, q], axis=0)
    for c in range(N_FSDP):
        head, rest = split(w_ref[c])
        pulled = dot(jnp.concatenate([head, rest], axis=0), twice, TN)
        scale = column_of(col_ref[c, 0:1, :], 256)
        value = pulled - scale * chunk_of(c, own_ref, other_ref).astype(F32)
        out_ref = keep_ref if c < 4 else give_ref
        out_ref[(c % 4) * 256 : (c % 4 + 1) * 256, :] = value


def forward_kernel(
    scalar_ref, t0, t1, t2, t3, t4, t5, t6, t7, weight_ref, cos_ref, sin_ref,
    q_ref, k_ref, v_ref, p_ref, csum_ref, low_ref, up_ref,
    tok, wv, acc, lacc, tok_sem, w_sem,
):
    tokens = (t0, t1, t2, t3, t4, t5, t6, t7)
    head = scalar_ref[0]
    tok_copies = [
        pltpu.make_async_copy(t, tok.at[pl.ds(L * n, L)], tok_sem.at[n]) for n, t in enumerate(tokens)
    ]
    w_copies = [
        pltpu.make_async_copy(weight_ref.at[n], wv.at[n], w_sem.at[n]) for n in range(N_FSDP)
    ]
    w_copies[0].start()
    tok_copies[0].start()
    tok_copies[1].start()
    for n in range(1, N_FSDP):
        w_copies[n].start()
    for n in range(2, N_FSDP):
        tok_copies[n].start()

    cos = cos_ref[...]
    sin = sin_ref[...]
    causal = lax.broadcasted_iota(jnp.int32, (L, L), 0) >= lax.broadcasted_iota(jnp.int32, (L, L), 1)
    causal = jnp.concatenate([causal.astype(F32)] * GROUP, axis=0) > 0.5

    def rope(x):
        return (x * cos + pltpu.roll(x, HD // 2, 1) * sin).astype(BF16)

    @pl.loop(0, 4)
    def _(i):
        for n in range(4):

            @pl.when(i == n)
            def _():
                tok_copies[2 * n].wait()
                tok_copies[2 * n + 1].wait()

        rows = pl.ds(pl.multiple_of(i * 2 * L, 2 * L), 2 * L)
        for n in range(N_FSDP):

            @pl.when(i == 0)
            def _():
                w_copies[n].wait()

            x = tok[rows, ROWS * n : ROWS * (n + 1)]
            part = dot(x, wv[n, 0:ROWS, :])
            low_part = dot(x, wv[n, ROWS : ROWS + LOW, 0:ROWS], NT)
            if n == 0:
                acc[...] = part
                lacc[...] = low_part
            else:
                acc[...] += part
                lacc[...] += low_part

        @pl.when(i == 0)
        def _():
            up_ref[...] = jnp.zeros_like(up_ref)
            for j in range(GROUP + 2):
                tile = GROUP * head + j if j < GROUP else (HQ + HK * (j - GROUP)) + head
                shard = tile // 3
                lanes = pl.ds(pl.multiple_of((tile % 3) * HD, HD), HD)
                block = max(0, j - GROUP + 1)
                up_ref[ADAPTER_RANK * block : ADAPTER_RANK * (block + 1), HD * j : HD * (j + 1)] = (
                    wv[shard, ROWS + LOW : ROWS + LOW + ADAPTER_RANK, lanes]
                )

        low = lacc[...].astype(BF16)
        acc[...] += ADAPTER_SCALE * dot(low, up_ref[...])
        for s in range(2):
            n = 2 * i + s
            r = slice(L * s, L * (s + 1))
            low_ref[n] = low[r]
            q = jnp.concatenate([rope(acc[r, HD * j : HD * (j + 1)]) for j in range(GROUP)], axis=0)
            k = rope(acc[r, GROUP * HD : (GROUP + 1) * HD])
            q_ref[n] = q
            k_ref[n] = k
            v_ref[n] = acc[r, (GROUP + 1) * HD : (GROUP + 2) * HD].astype(BF16)
            scores = dot(q, k, NT) / math.sqrt(HD)
            scores = jnp.where(causal, scores, -1e30)
            e = jnp.exp(scores - jnp.max(scores, axis=1, keepdims=True))
            p = e / jnp.sum(e, axis=1, keepdims=True)
            p_ref[n] = p
            rounded = p.astype(BF16).astype(F32)
            csum_ref[n] = jnp.zeros((8, L), F32)
            for j in range(GROUP):
                csum_ref[n, j : j + 1, :] = jnp.sum(rounded[L * j : L * (j + 1)], axis=0, keepdims=True)


def forward(scalars, tokens, weight, cos, sin):
    n = len(tokens)
    return pl.pallas_call(
        forward_kernel,
        name="attention_forward",
        in_specs=[SMEM] + [ANY] * (n + 1) + [VMEM, VMEM],
        out_specs=[VMEM] * 7,
        out_shape=[
            jax.ShapeDtypeStruct((n, GROUP * L, HD), BF16),
            jax.ShapeDtypeStruct((n, L, HD), BF16),
            jax.ShapeDtypeStruct((n, L, HD), BF16),
            jax.ShapeDtypeStruct((n, GROUP * L, L), F32),
            jax.ShapeDtypeStruct((n, 8, L), F32),
            jax.ShapeDtypeStruct((n, L, LOW), BF16),
            jax.ShapeDtypeStruct((LOW, COLS), BF16),
        ],
        scratch_shapes=[
            pltpu.VMEM((n * L, MODEL_WIDTH), BF16),
            pltpu.VMEM((N_FSDP, ROWS + PACK, COLS), BF16),
            pltpu.VMEM((2 * L, COLS), F32),
            pltpu.VMEM((2 * L, LOW), F32),
            pltpu.SemaphoreType.DMA((n,)),
            pltpu.SemaphoreType.DMA((N_FSDP,)),
        ],
        compiler_params=params(),
        cost_estimate=cost(2 * n * L * MODEL_WIDTH * (COLS + LOW), 20e6),
    )(scalars, *tokens, weight, cos, sin)


def backward_kernel(
    scalar_ref, t0, t1, t2, t3, t4, t5, t6, t7, g_own, g_other, q_ref, k_ref, v_ref, p_ref,
    csum_ref, low_ref, up_ref, cos_ref, sin_ref, out_ref, tok, dlow, dup, g_all, tok_sem,
):
    tokens = (t0, t1, t2, t3, t4, t5, t6, t7)
    head = scalar_ref[0]
    core = scalar_ref[1]
    copies = [
        pltpu.make_async_copy(t, tok.at[pl.ds(L * n, L)], tok_sem.at[n]) for n, t in enumerate(tokens)
    ]
    for copy in copies:
        copy.start()
    cos = cos_ref[...]
    sin = sin_ref[...]
    up = up_ref[...]
    g_all[...] = jnp.zeros_like(g_all)
    shard_row = lax.broadcasted_iota(jnp.int32, (N_FSDP, 256), 0)
    for n in range(8):
        ref = (g_own, g_other)[(n // 2) % 2]
        rows = ref[(n // 4) * 2 + n % 2] / L
        for j in range(2):
            row = jnp.sum(jnp.where(shard_row == 2 * head + j, rows, 0.0), axis=0, keepdims=True)
            g_all[n, 2 * j : 2 * j + 1, :] = row[:, 0:HD]
            g_all[n, 2 * j + 1 : 2 * j + 2, :] = row[:, HD : 2 * HD]
    dup[...] = jnp.zeros_like(dup)

    def unrope(x):
        return x * cos + pltpu.roll(x * sin, HD // 2, 1)

    @pl.loop(0, 8)
    def _(n):
        g = g_all[n]
        g_head, g_rest = split(g)
        v = v_ref[n]
        k = k_ref[n]
        q = q_ref[n]
        u = dot(jnp.concatenate([g_head, g_rest], axis=0), v, NT)
        u = u[0:8] + u[8:16]
        parts = []
        for j in range(GROUP):
            p = p_ref[n, L * j : L * (j + 1), :]
            pu = p * u[j : j + 1]
            parts.append((pu - p * jnp.sum(pu, axis=1, keepdims=True)) * (1.0 / math.sqrt(HD)))
        ds_head, ds_rest = split(jnp.concatenate(parts, axis=0))
        dq = dot(ds_head, k) + dot(ds_rest, k)
        dk = dot(ds_head, q, TN) + dot(ds_rest, q, TN)
        c_head, c_rest = split(csum_ref[n])
        dv = dot(
            jnp.concatenate([c_head, c_rest, c_head, c_rest], axis=0),
            jnp.concatenate([g_head, g_head, g_rest, g_rest], axis=0),
            TN,
        )
        dproj = jnp.concatenate(
            [unrope(dq[L * j : L * (j + 1)]) for j in range(GROUP)] + [unrope(dk), dv], axis=1
        )
        head_part, rest_part = split(ADAPTER_SCALE * dproj)
        low_grad = dot(up, head_part, NT) + dot(up, rest_part, NT)
        l_head, l_rest = split(low_grad)
        lanes = pl.ds(pl.multiple_of(n * L, L), L)
        dlow[0:LOW, lanes] = l_head
        dlow[LOW : 2 * LOW, lanes] = l_rest
        low = low_ref[n]
        dup[...] += dot(low, head_part, TN) + dot(low, rest_part, TN)

    for half in range(2):
        spot = core if half == 0 else 1 - core
        if half == 1:
            out_ref[pl.ds(spot, 1), RING // 2 : RING] = jnp.zeros((1, RING // 2, N_FSDP, 8, HD), F32)
    far = 1 - core
    for j in range(GROUP + 2):
        tile = GROUP * head + j if j < GROUP else (HQ + HK * (j - GROUP)) + head
        shard = tile // 3
        block = max(0, j - GROUP + 1)
        value = dup[ADAPTER_RANK * block : ADAPTER_RANK * (block + 1), HD * j : HD * (j + 1)]
        for i in range(2):
            out_ref[far, RING // 2 + 2 * (tile % 3) + i, shard] = value[8 * i : 8 * (i + 1)]
    for copy in copies:
        copy.wait()
    for f in range(N_FSDP):
        both = dot(dlow[...], tok[:, ROWS * f : ROWS * (f + 1)])
        value = both[0:LOW] + both[LOW : 2 * LOW]
        for b in range(ROWS // HD):
            for i in range(LOW // 8):
                group = b * (LOW // 8) + i
                spot = core if group < RING else 1 - core
                out_ref[spot, group % RING, f] = value[8 * i : 8 * (i + 1), HD * b : HD * (b + 1)]


def backward(scalars, tokens, g_own, g_other, saved, cos, sin):
    n = len(tokens)
    return pl.pallas_call(
        backward_kernel,
        name="attention_backward",
        in_specs=[SMEM] + [ANY] * n + [VMEM] * 11,
        out_specs=VMEM,
        out_shape=jax.ShapeDtypeStruct((2, RING, N_FSDP, 8, HD), F32),
        scratch_shapes=[
            pltpu.VMEM((n * L, MODEL_WIDTH), BF16),
            pltpu.VMEM((2 * LOW, n * L), BF16),
            pltpu.VMEM((LOW, COLS), F32),
            pltpu.VMEM((n, 8, HD), F32),
            pltpu.SemaphoreType.DMA((n,)),
        ],
        compiler_params=params(),
        cost_estimate=cost(2 * n * L * MODEL_WIDTH * 2 * LOW, 15e6),
    )(scalars, *tokens, g_own, g_other, *saved, cos, sin)


def finish_kernel(scalar_ref, own_ref, other_ref, down_ref, up_ref):
    core = scalar_ref[1]
    squares = jnp.sum(own_ref[:, 8:9, :], axis=0) + jnp.sum(other_ref[:, 8:9, :], axis=0)
    grad_norm = jnp.sqrt(jnp.sum(squares, axis=1, keepdims=True))
    unit_scale = math.sqrt(3 * MODEL_WIDTH * ADAPTER_RANK + (HQ + 2 * HK) * HD * ADAPTER_RANK)
    factor = jnp.minimum(1.0, MAX_NORM / (grad_norm + 1e-06)) * unit_scale

    def tile(group):
        half, spot = divmod(group, RING)
        a = own_ref[spot, 0:8, :]
        b = other_ref[spot, 0:8, :]
        return jnp.where(core == half, a, b) * factor

    for b in range(ROWS // HD):
        for i in range(LOW // 8):
            down_ref[8 * i : 8 * (i + 1), HD * b : HD * (b + 1)] = tile(b * (LOW // 8) + i)
    for b in range(UP_ROWS // HD):
        for i in range(ADAPTER_RANK // 8):
            group = (ROWS // HD) * (LOW // 8) + 2 * b + i
            up_ref[8 * i : 8 * (i + 1), HD * b : HD * (b + 1)] = tile(group)


def dp_pairs(move):
    pairs = []
    for d in range(N_DP):
        z, y, core = move(d // 4, (d // 2) % 2, d % 2)
        pairs.append((d, (z % (N_DP // 4)) * 4 + y * 2 + core))
    return pairs


SIBLING = dp_pairs(lambda z, y, c: (z, y, 1 - c))
UPWARD = dp_pairs(lambda z, y, c: (z + 1, y, c))
DOWNWARD = dp_pairs(lambda z, y, c: (z - 1, y, c))
CORE_GROUPS = [[2 * i + c for i in range(RING)] for c in range(2)]


def to_sibling(x):
    return lax.ppermute(x, "dp", SIBLING)


def swap_dp(x):
    return lax.all_to_all(x, "dp", 0, 0, axis_index_groups=CORE_GROUPS)


def swap_fsdp(x):
    return lax.all_to_all(x, "fsdp", 0, 0)


def shards(
    query_rows, passage_rows, positive, layer_input, gain, frozen_weight, down_maps, up_maps
):
    dp = lax.axis_index("dp")
    core = dp % 2
    head = 2 * ((dp // 4) % 2) + core
    scalars = jnp.stack([head, core]).astype(jnp.int32)
    cos, sin = (jnp.asarray(t) for t in rope_tables())

    columns = [
        lax.dynamic_slice_in_dim(frozen_weight, GROUP * HD * head, GROUP * HD, 1),
        lax.dynamic_slice_in_dim(frozen_weight, HQ * HD + HD * head, HD, 1),
        lax.dynamic_slice_in_dim(frozen_weight, (HQ + HK) * HD + HD * head, HD, 1),
    ]
    packed = jnp.concatenate(
        [
            jnp.concatenate(columns, axis=1),
            jnp.pad(down_maps.T, ((0, 0), (0, COLS - ROWS))),
            jnp.pad(up_maps.T, ((0, 0), (0, COLS - UP_ROWS))),
        ],
        axis=0,
    )
    weight = lax.all_gather(packed, "fsdp", axis=0)

    first, second = normalize(layer_input, gain)
    from_below = lax.ppermute(first, "dp", UPWARD)
    from_above = lax.ppermute(second, "dp", DOWNWARD)
    tokens = [first, second, to_sibling(first), to_sibling(second)]
    tokens += [from_below, from_above, to_sibling(from_below), to_sibling(from_above)]

    own = swap_dp(jnp.broadcast_to(passage_rows[None], (RING, 64, 256))).reshape(RING * 64, 256)
    other = to_sibling(own)
    partial = pl.pallas_call(
        partial_scores_kernel,
        name="partial_scores",
        out_shape=jax.ShapeDtypeStruct((N_FSDP, 72, 256), F32),
        compiler_params=params(),
        cost_estimate=cost(2 * 64 * 256 * 2048 * 2, 2e6),
    )(query_rows, own, other)
    scores = pl.pallas_call(
        finish_scores_kernel,
        name="finish_scores",
        out_shape=jax.ShapeDtypeStruct((N_FSDP, 72, 256), F32),
        compiler_params=params(),
        cost_estimate=cost(64 * 256 * 20, 1.2e6),
    )(swap_fsdp(partial))
    scores = swap_fsdp(scores)
    owner = positive // 64
    place = (
        jnp.where(owner % 2 == core, 0, RING * 64) + (owner // 2) * 64 + positive % 64
    ).astype(jnp.int32)
    query_grad, pulls, columns_sum = pl.pallas_call(
        query_grad_kernel,
        name="query_grad",
        out_shape=[
            jax.ShapeDtypeStruct((64, 256), F32),
            jax.ShapeDtypeStruct((N_FSDP, 64, 256), F32),
            jax.ShapeDtypeStruct((N_FSDP, 8, 256), F32),
        ],
        compiler_params=params(),
        cost_estimate=cost(2 * 128 * 256 * 2048, 2e6),
    )(scores, query_rows, place.reshape(64, 1), own, other)
    g = swap_fsdp(query_grad[:16].reshape(N_FSDP, 2, 256))
    g = jnp.swapaxes(g, 0, 1)
    g_own = jnp.concatenate(
        [g, lax.ppermute(g[0:1], "dp", UPWARD), lax.ppermute(g[1:2], "dp", DOWNWARD)], axis=0
    )
    g_other = to_sibling(g_own)

    keep, give = pl.pallas_call(
        passage_terms_kernel,
        name="passage_terms",
        out_shape=[jax.ShapeDtypeStruct((RING * 64, 256), F32)] * 2,
        compiler_params=params(),
        cost_estimate=cost(2 * 128 * 256 * 2048, 6e6),
    )(pulls, columns_sum, query_rows, own, other)
    sent = (keep + to_sibling(give)).astype(BF16).reshape(RING, 64, 256)
    passage_grad = jnp.sum(swap_dp(sent).astype(F32), axis=0)

    *saved, = forward(scalars, tokens, weight, cos, sin)
    grads = backward(scalars, tokens, g_own, g_other, saved, cos, sin)
    summed = (grads[0] + to_sibling(grads[1])).astype(BF16)
    piece = jnp.sum(swap_dp(summed).astype(F32), axis=0)
    pieces = jnp.sum(swap_fsdp(jnp.broadcast_to(piece[None], (N_FSDP,) + piece.shape)), axis=0)
    squares = jnp.sum(pieces * pieces, axis=(0, 1))
    mine = lax.dynamic_index_in_dim(pieces, lax.axis_index("fsdp"), 0, keepdims=False)
    tail = jnp.concatenate([mine, jnp.broadcast_to(squares[None], (8, HD))], axis=0)
    tail_own = swap_dp(jnp.broadcast_to(tail[None], (RING, 16, HD)))
    tail_other = to_sibling(tail_own)
    down, up = pl.pallas_call(
        finish_kernel,
        name="finish_clip",
        in_specs=[SMEM, VMEM, VMEM],
        out_shape=[
            jax.ShapeDtypeStruct((LOW, ROWS), F32),
            jax.ShapeDtypeStruct((ADAPTER_RANK, UP_ROWS), F32),
        ],
        compiler_params=params(),
    )(scalars, tail_own, tail_other)
    return query_grad, passage_grad, down.T, up.T


def solution(mesh):
    in_specs = (
        P("dp", "fsdp"),
        P("dp", "fsdp"),
        P("dp"),
        P(("dp", "fsdp"), None, None),
        P(),
        P("fsdp", None),
        P("fsdp", None),
        P("fsdp", None),
    )
    out_specs = (P("dp", "fsdp"), P("dp", "fsdp"), P("fsdp", None), P("fsdp", None))
    return jax.shard_map(shards, mesh=mesh, in_specs=in_specs, out_specs=out_specs, check_vma=False)
```

```python
import functools
import math

import jax
import jax.numpy as jnp
import numpy as np
from jax import lax
from jax.experimental import pallas as pl
from jax.experimental.pallas import tpu as pltpu
from jax.sharding import PartitionSpec as P

MODEL_WIDTH = 4096
HD = 128
HQ = 16
HK = 4
GROUP = HQ // HK
ADAPTER_RANK = 16
L = 128
EPS_NORM = 1e-06
SOFTMAX_TEMPER = 0.02
ADAPTER_SCALE = 2.0
RMS_EPS = 1e-05
ROPE_BASE = 10000.0
MAX_NORM = 1.0

N_DP = 32
N_FSDP = 8
RING = N_DP // 2
ROWS = MODEL_WIDTH // N_FSDP
UP_ROWS = (HQ + 2 * HK) * HD // N_FSDP
COLS = (GROUP + 2) * HD
PACK = 3 * ADAPTER_RANK + ADAPTER_RANK
LOW = 3 * ADAPTER_RANK
F32 = jnp.float32
BF16 = jnp.bfloat16
VMEM_LIMIT = 48 * 1024 * 1024

NN = (((1,), (0,)), ((), ()))
NT = (((1,), (1,)), ((), ()))
TN = (((0,), (0,)), ((), ()))


def dot(a, b, dims=NN):
    return lax.dot_general(a, b, dims, preferred_element_type=F32)


def split(x):
    head = x.astype(BF16)
    return head, (x - head.astype(F32)).astype(BF16)


def params():
    return pltpu.CompilerParams(vmem_limit_bytes=VMEM_LIMIT)


def cost(flops, bytes_accessed):
    return pl.CostEstimate(flops=int(flops), bytes_accessed=int(bytes_accessed), transcendentals=0)


VMEM = pl.BlockSpec(memory_space=pltpu.VMEM)
SMEM = pl.BlockSpec(memory_space=pltpu.SMEM)
ANY = pl.BlockSpec(memory_space=pl.ANY)


def rope_tables():
    half = HD // 2
    freqs = np.power(
        np.float32(ROPE_BASE), -(np.arange(half, dtype=np.float32) * np.float32(2.0)) / np.float32(HD)
    ).astype(np.float32)
    angles = np.arange(L, dtype=np.float32)[:, None] * freqs[None, :]
    cosine = np.cos(angles).astype(np.float32)
    sine = np.sin(angles).astype(np.float32)
    return np.concatenate([cosine, cosine], 1), np.concatenate([-sine, sine], 1)


def normalize_kernel(x_ref, gain_ref, first_ref, second_ref):
    for s, out_ref in enumerate((first_ref, second_ref)):
        values = x_ref[s].astype(F32)
        scale = lax.rsqrt(jnp.mean(values * values, axis=-1, keepdims=True) + RMS_EPS)
        out_ref[...] = (values * scale * gain_ref[...]).astype(BF16)


def normalize(x, gain):
    shape = jax.ShapeDtypeStruct((L, MODEL_WIDTH), BF16)
    step = 32
    return pl.pallas_call(
        normalize_kernel,
        name="normalize",
        grid=(L // step,),
        in_specs=[
            pl.BlockSpec((2, step, MODEL_WIDTH), lambda i: (0, i, 0)),
            pl.BlockSpec((1, MODEL_WIDTH), lambda i: (0, 0)),
        ],
        out_specs=[pl.BlockSpec((step, MODEL_WIDTH), lambda i: (i, 0))] * 2,
        out_shape=[shape, shape],
        compiler_params=params(),
        cost_estimate=cost(6 * 2 * L * MODEL_WIDTH, 8 * L * MODEL_WIDTH),
    )(x, gain.reshape(1, MODEL_WIDTH))


def eye_mask(n, m):
    return lax.broadcasted_iota(jnp.int32, (n, m), 0) == lax.broadcasted_iota(jnp.int32, (n, m), 1)


def column_of(row, n):
    return jnp.sum(jnp.where(eye_mask(n, row.shape[1]), row, 0.0), axis=1, keepdims=True)


def chunk_of(c, own_ref, other_ref, size=256):
    per = own_ref.shape[0] // size
    ref = own_ref if c < per else other_ref
    return ref[(c % per) * size : (c % per + 1) * size, :]


def partial_scores_kernel(q_ref, own_ref, other_ref, out_ref):
    q = q_ref[...]
    ones = jnp.ones((16, 256), BF16)
    rows = lax.broadcasted_iota(jnp.int32, (8, 256), 0)

    def square_row(block):
        values = block.astype(F32)
        head, rest = split(values * values)
        return (dot(ones, head, NT) + dot(ones, rest, NT))[0:8]

    q_row = square_row(jnp.concatenate([q, jnp.zeros((256 - 64, 256), BF16)], axis=0))
    for c in range(N_FSDP):
        passages = chunk_of(c, own_ref, other_ref)
        out_ref[c, 0:64, :] = dot(q, passages, NT)
        out_ref[c, 64:72, :] = jnp.where(
            rows == 0, square_row(passages), jnp.where(rows == 1, q_row, 0.0)
        )


def finish_scores_kernel(parts_ref, out_ref):
    total = parts_ref[0]
    for c in range(1, N_FSDP):
        total = total + parts_ref[c]
    p_norm = jnp.sqrt(total[64:65] + EPS_NORM)
    q_norm_row = jnp.sqrt(total[65:66] + EPS_NORM)
    q_norm = column_of(q_norm_row, 64)
    scores = total[0:64] / (q_norm * p_norm * SOFTMAX_TEMPER)
    rows = lax.broadcasted_iota(jnp.int32, (8, 256), 0)
    tail = jnp.where(rows == 0, p_norm, jnp.where(rows == 1, q_norm_row, 0.0))
    for c in range(N_FSDP):
        out_ref[c, 0:64, :] = scores
        out_ref[c, 64:72, :] = tail


def query_grad_kernel(s_ref, q_ref, pos_ref, own_ref, other_ref, grad_ref, w_ref, col_ref, rerun_ref):
    top = jnp.max(s_ref[0, 0:64, :], axis=1, keepdims=True)
    for c in range(1, N_FSDP):
        top = jnp.maximum(top, jnp.max(s_ref[c, 0:64, :], axis=1, keepdims=True))
    norm = jnp.zeros((64, 1), F32)
    for c in range(N_FSDP):
        norm = norm + jnp.sum(jnp.exp(s_ref[c, 0:64, :] - top), axis=1, keepdims=True)
    q_norm = column_of(s_ref[0, 65:66, :], 64)
    place = pos_ref[...]
    lane = lax.broadcasted_iota(jnp.int32, (64, 256), 1)
    cross = jnp.zeros((64, 1), F32)
    total = jnp.zeros((64, 256), F32)
    for c in range(N_FSDP):
        s = s_ref[c, 0:64, :]
        p_norm = s_ref[c, 64:65, :]
        grad = jnp.exp(s - top) / norm - jnp.where(lane + 256 * c == place, 1.0, 0.0)
        terms = grad * s
        cross = cross + jnp.sum(terms, axis=1, keepdims=True)
        column = jnp.sum(terms, axis=0, keepdims=True)
        col_ref[c] = jnp.broadcast_to(column / (p_norm * p_norm), (8, 256))
        weight = grad / (p_norm * SOFTMAX_TEMPER)
        w_ref[c] = weight / q_norm
        head, rest = split(weight)
        both = dot(jnp.concatenate([head, rest], axis=0), chunk_of(c, own_ref, other_ref))
        total = total + both[0:64] + both[64:128]
    query_grad = total / q_norm - (cross / (q_norm * q_norm)) * q_ref[...].astype(F32)
    grad_ref[...] = query_grad
    for m in range(N_FSDP):
        rerun_ref[m] = query_grad[2 * m : 2 * m + 2]


def passage_terms_kernel(w_ref, col_ref, q_ref, own_ref, other_ref, keep_ref, give_ref):
    q = q_ref[...]
    twice = jnp.concatenate([q, q], axis=0)
    for c in range(N_FSDP):
        head, rest = split(w_ref[c])
        pulled = dot(jnp.concatenate([head, rest], axis=0), twice, TN)
        scale = column_of(col_ref[c, 0:1, :], 256)
        value = pulled - scale * chunk_of(c, own_ref, other_ref).astype(F32)
        out_ref = keep_ref if c < 4 else give_ref
        out_ref[(c % 4) * 256 : (c % 4 + 1) * 256, :] = value


def project_kernel(
    scalar_ref, t0, t1, t2, t3, t4, t5, t6, t7, weight_ref, cos_ref, sin_ref,
    q_ref, k_ref, v_ref, low_ref, up_ref,
    tok, wv, acc, lacc, tok_sem, w_sem,
):
    tokens = (t0, t1, t2, t3, t4, t5, t6, t7)
    head = scalar_ref[0]
    tok_copies = [
        pltpu.make_async_copy(t, tok.at[pl.ds(L * n, L)], tok_sem.at[n]) for n, t in enumerate(tokens)
    ]
    w_copies = [
        pltpu.make_async_copy(weight_ref.at[n], wv.at[n], w_sem.at[n]) for n in range(N_FSDP)
    ]
    w_copies[0].start()
    tok_copies[0].start()
    tok_copies[1].start()
    for n in range(1, N_FSDP):
        w_copies[n].start()
    for n in range(2, N_FSDP):
        tok_copies[n].start()

    cos = cos_ref[...]
    sin = sin_ref[...]
    def rope(x):
        return (x * cos + pltpu.roll(x, HD // 2, 1) * sin).astype(BF16)

    @pl.loop(0, 4)
    def _(i):
        for n in range(4):

            @pl.when(i == n)
            def _():
                tok_copies[2 * n].wait()
                tok_copies[2 * n + 1].wait()

        rows = pl.ds(pl.multiple_of(i * 2 * L, 2 * L), 2 * L)
        for n in range(N_FSDP):

            @pl.when(i == 0)
            def _():
                w_copies[n].wait()

            x = tok[rows, ROWS * n : ROWS * (n + 1)]
            part = dot(x, wv[n, 0:ROWS, :])
            low_part = dot(x, wv[n, ROWS : ROWS + LOW, 0:ROWS], NT)
            if n == 0:
                acc[...] = part
                lacc[...] = low_part
            else:
                acc[...] += part
                lacc[...] += low_part

        @pl.when(i == 0)
        def _():
            up_ref[...] = jnp.zeros_like(up_ref)
            for j in range(GROUP + 2):
                tile = GROUP * head + j if j < GROUP else (HQ + HK * (j - GROUP)) + head
                shard = tile // 3
                lanes = pl.ds(pl.multiple_of((tile % 3) * HD, HD), HD)
                block = max(0, j - GROUP + 1)
                up_ref[ADAPTER_RANK * block : ADAPTER_RANK * (block + 1), HD * j : HD * (j + 1)] = (
                    wv[shard, ROWS + LOW : ROWS + LOW + ADAPTER_RANK, lanes]
                )

        low = lacc[...].astype(BF16)
        acc[...] += ADAPTER_SCALE * dot(low, up_ref[...])
        for s in range(2):
            n = 2 * i + s
            r = slice(L * s, L * (s + 1))
            low_ref[n] = low[r]
            q = jnp.concatenate([rope(acc[r, HD * j : HD * (j + 1)]) for j in range(GROUP)], axis=0)
            k = rope(acc[r, GROUP * HD : (GROUP + 1) * HD])
            q_ref[n] = q
            k_ref[n] = k
            v_ref[n] = acc[r, (GROUP + 1) * HD : (GROUP + 2) * HD].astype(BF16)


def project(scalars, tokens, weight, cos, sin):
    n = len(tokens)
    return pl.pallas_call(
        project_kernel,
        name="project",
        in_specs=[SMEM] + [ANY] * (n + 1) + [VMEM, VMEM],
        out_specs=[VMEM] * 5,
        out_shape=[
            jax.ShapeDtypeStruct((n, GROUP * L, HD), BF16),
            jax.ShapeDtypeStruct((n, L, HD), BF16),
            jax.ShapeDtypeStruct((n, L, HD), BF16),
            jax.ShapeDtypeStruct((n, L, LOW), BF16),
            jax.ShapeDtypeStruct((LOW, COLS), BF16),
        ],
        scratch_shapes=[
            pltpu.VMEM((n * L, MODEL_WIDTH), BF16),
            pltpu.VMEM((N_FSDP, ROWS + PACK, COLS), BF16),
            pltpu.VMEM((2 * L, COLS), F32),
            pltpu.VMEM((2 * L, LOW), F32),
            pltpu.SemaphoreType.DMA((n,)),
            pltpu.SemaphoreType.DMA((N_FSDP,)),
        ],
        compiler_params=params(),
        cost_estimate=cost(2 * n * L * MODEL_WIDTH * (COLS + LOW), 20e6),
    )(scalars, *tokens, weight, cos, sin)


def attend_kernel(q_ref, k_ref, p_ref, csum_ref):
    causal = lax.broadcasted_iota(jnp.int32, (L, L), 0) >= lax.broadcasted_iota(jnp.int32, (L, L), 1)
    causal = jnp.concatenate([causal.astype(F32)] * GROUP, axis=0) > 0.5

    @pl.loop(0, q_ref.shape[0])
    def _(n):
        scores = dot(q_ref[n], k_ref[n], NT) / math.sqrt(HD)
        scores = jnp.where(causal, scores, -1e30)
        e = jnp.exp(scores - jnp.max(scores, axis=1, keepdims=True))
        p = e / jnp.sum(e, axis=1, keepdims=True)
        p_ref[n] = p
        rounded = p.astype(BF16).astype(F32)
        csum_ref[n] = jnp.zeros((8, L), F32)
        for j in range(GROUP):
            csum_ref[n, j : j + 1, :] = jnp.sum(rounded[L * j : L * (j + 1)], axis=0, keepdims=True)


def attend(queries, keys):
    n = queries.shape[0]
    return pl.pallas_call(
        attend_kernel,
        name="attend",
        in_specs=[VMEM, VMEM],
        out_specs=[VMEM, VMEM],
        out_shape=[
            jax.ShapeDtypeStruct((n, GROUP * L, L), F32),
            jax.ShapeDtypeStruct((n, 8, L), F32),
        ],
        compiler_params=params(),
        cost_estimate=cost(2 * n * GROUP * L * L * HD * 10, 4e6),
    )(queries, keys)


def backward_kernel(
    scalar_ref, t0, t1, t2, t3, t4, t5, t6, t7, g_own, g_other, q_ref, k_ref, v_ref, p_ref,
    csum_ref, low_ref, up_ref, cos_ref, sin_ref, out_ref, tok, dlow, dup, g_all, tok_sem,
):
    tokens = (t0, t1, t2, t3, t4, t5, t6, t7)
    head = scalar_ref[0]
    core = scalar_ref[1]
    copies = [
        pltpu.make_async_copy(t, tok.at[pl.ds(L * n, L)], tok_sem.at[n]) for n, t in enumerate(tokens)
    ]
    for copy in copies:
        copy.start()
    cos = cos_ref[...]
    sin = sin_ref[...]
    up = up_ref[...]
    g_all[...] = jnp.zeros_like(g_all)
    shard_row = lax.broadcasted_iota(jnp.int32, (N_FSDP, 256), 0)
    for n in range(8):
        ref = (g_own, g_other)[(n // 2) % 2]
        rows = ref[(n // 4) * 2 + n % 2] / L
        for j in range(2):
            row = jnp.sum(jnp.where(shard_row == 2 * head + j, rows, 0.0), axis=0, keepdims=True)
            g_all[n, 2 * j : 2 * j + 1, :] = row[:, 0:HD]
            g_all[n, 2 * j + 1 : 2 * j + 2, :] = row[:, HD : 2 * HD]
    dup[...] = jnp.zeros_like(dup)

    def unrope(x):
        return x * cos + pltpu.roll(x * sin, HD // 2, 1)

    @pl.loop(0, 8)
    def _(n):
        g = g_all[n]
        g_head, g_rest = split(g)
        v = v_ref[n]
        k = k_ref[n]
        q = q_ref[n]
        u = dot(jnp.concatenate([g_head, g_rest], axis=0), v, NT)
        u = u[0:8] + u[8:16]
        parts = []
        for j in range(GROUP):
            p = p_ref[n, L * j : L * (j + 1), :]
            pu = p * u[j : j + 1]
            parts.append((pu - p * jnp.sum(pu, axis=1, keepdims=True)) * (1.0 / math.sqrt(HD)))
        ds_head, ds_rest = split(jnp.concatenate(parts, axis=0))
        dq = dot(ds_head, k) + dot(ds_rest, k)
        dk = dot(ds_head, q, TN) + dot(ds_rest, q, TN)
        c_head, c_rest = split(csum_ref[n])
        dv = dot(
            jnp.concatenate([c_head, c_rest, c_head, c_rest], axis=0),
            jnp.concatenate([g_head, g_head, g_rest, g_rest], axis=0),
            TN,
        )
        dproj = jnp.concatenate(
            [unrope(dq[L * j : L * (j + 1)]) for j in range(GROUP)] + [unrope(dk), dv], axis=1
        )
        head_part, rest_part = split(ADAPTER_SCALE * dproj)
        low_grad = dot(up, head_part, NT) + dot(up, rest_part, NT)
        l_head, l_rest = split(low_grad)
        lanes = pl.ds(pl.multiple_of(n * L, L), L)
        dlow[0:LOW, lanes] = l_head
        dlow[LOW : 2 * LOW, lanes] = l_rest
        low = low_ref[n]
        dup[...] += dot(low, head_part, TN) + dot(low, rest_part, TN)

    far = 1 - core
    out_ref[pl.ds(far, 1), :, RING // 2 : RING] = jnp.zeros((1, N_FSDP, RING // 2, 8, HD), F32)
    for j in range(GROUP + 2):
        tile = GROUP * head + j if j < GROUP else (HQ + HK * (j - GROUP)) + head
        shard = tile // 3
        block = max(0, j - GROUP + 1)
        value = dup[ADAPTER_RANK * block : ADAPTER_RANK * (block + 1), HD * j : HD * (j + 1)]
        for i in range(2):
            out_ref[far, shard, RING // 2 + 2 * (tile % 3) + i] = value[8 * i : 8 * (i + 1)]
    for copy in copies:
        copy.wait()
    for f in range(N_FSDP):
        both = dot(dlow[...], tok[:, ROWS * f : ROWS * (f + 1)])
        value = both[0:LOW] + both[LOW : 2 * LOW]
        for b in range(ROWS // HD):
            for i in range(LOW // 8):
                group = b * (LOW // 8) + i
                spot = core if group < RING else 1 - core
                out_ref[spot, f, group % RING] = value[8 * i : 8 * (i + 1), HD * b : HD * (b + 1)]


def backward(scalars, tokens, g_own, g_other, saved, cos, sin):
    n = len(tokens)
    return pl.pallas_call(
        backward_kernel,
        name="attention_backward",
        in_specs=[SMEM] + [ANY] * n + [VMEM] * 11,
        out_specs=VMEM,
        out_shape=jax.ShapeDtypeStruct((2, N_FSDP, RING, 8, HD), F32),
        scratch_shapes=[
            pltpu.VMEM((n * L, MODEL_WIDTH), BF16),
            pltpu.VMEM((2 * LOW, n * L), BF16),
            pltpu.VMEM((LOW, COLS), F32),
            pltpu.VMEM((n, 8, HD), F32),
            pltpu.SemaphoreType.DMA((n,)),
        ],
        compiler_params=params(),
        cost_estimate=cost(2 * n * L * MODEL_WIDTH * 2 * LOW, 15e6),
    )(scalars, *tokens, g_own, g_other, *saved, cos, sin)


def fold_kernel(parts_ref, out_ref):
    total = parts_ref[0]
    for n in range(1, N_FSDP):
        total = total + parts_ref[n]
    total = total.astype(BF16)
    for n in range(RING):
        out_ref[n] = total


def total_kernel(parts_ref, out_ref, squares_ref):
    total = parts_ref[0].astype(F32)
    for n in range(1, RING):
        total = total + parts_ref[n].astype(F32)
    out_ref[...] = total
    squares = jnp.broadcast_to(jnp.sum(total * total, axis=0, keepdims=True), (8, HD))
    for n in range(N_FSDP):
        squares_ref[n] = squares


def finish_kernel(scalar_ref, own_ref, other_ref, squares_ref, squares_other_ref, down_ref, up_ref):
    core = scalar_ref[1]
    squares = jnp.sum(squares_ref[:, 0:1, :], axis=0) + jnp.sum(squares_other_ref[:, 0:1, :], axis=0)
    grad_norm = jnp.sqrt(jnp.sum(squares, axis=1, keepdims=True))
    unit_scale = math.sqrt(3 * MODEL_WIDTH * ADAPTER_RANK + (HQ + 2 * HK) * HD * ADAPTER_RANK)
    factor = jnp.minimum(1.0, MAX_NORM / (grad_norm + 1e-06)) * unit_scale

    def tile(group):
        half, spot = divmod(group, RING)
        a = own_ref[8 * spot : 8 * spot + 8, :]
        b = other_ref[8 * spot : 8 * spot + 8, :]
        return jnp.where(core == half, a, b) * factor

    for b in range(ROWS // HD):
        for i in range(LOW // 8):
            down_ref[8 * i : 8 * (i + 1), HD * b : HD * (b + 1)] = tile(b * (LOW // 8) + i)
    for b in range(UP_ROWS // HD):
        for i in range(ADAPTER_RANK // 8):
            group = (ROWS // HD) * (LOW // 8) + 2 * b + i
            up_ref[8 * i : 8 * (i + 1), HD * b : HD * (b + 1)] = tile(group)


def dp_pairs(move):
    pairs = []
    for d in range(N_DP):
        z, y, core = move(d // 4, (d // 2) % 2, d % 2)
        pairs.append((d, (z % (N_DP // 4)) * 4 + y * 2 + core))
    return pairs


SIBLING = dp_pairs(lambda z, y, c: (z, y, 1 - c))
UPWARD = dp_pairs(lambda z, y, c: (z + 1, y, c))
DOWNWARD = dp_pairs(lambda z, y, c: (z - 1, y, c))
CORE_GROUPS = [[2 * i + c for i in range(RING)] for c in range(2)]


def to_sibling(x):
    return lax.ppermute(x, "dp", SIBLING)


def after(x, *others):
    return lax.optimization_barrier((x,) + others)[0]


def swap_dp(x):
    return lax.all_to_all(x, "dp", 0, 0, axis_index_groups=CORE_GROUPS)


def swap_fsdp(x):
    return lax.all_to_all(x, "fsdp", 0, 0)


def shards(
    query_rows, passage_rows, positive, layer_input, gain, frozen_weight, down_maps, up_maps
):
    dp = lax.axis_index("dp")
    core = dp % 2
    head = 2 * ((dp // 4) % 2) + core
    cos, sin = (jnp.asarray(t) for t in rope_tables())

    scalars = jnp.stack([head, core]).astype(jnp.int32)
    columns = [
        lax.dynamic_slice_in_dim(frozen_weight, GROUP * HD * head, GROUP * HD, 1),
        lax.dynamic_slice_in_dim(frozen_weight, HQ * HD + HD * head, HD, 1),
        lax.dynamic_slice_in_dim(frozen_weight, (HQ + HK) * HD + HD * head, HD, 1),
    ]
    packed = jnp.concatenate(
        [
            jnp.concatenate(columns, axis=1),
            jnp.pad(down_maps.T, ((0, 0), (0, COLS - ROWS))),
            jnp.pad(up_maps.T, ((0, 0), (0, COLS - UP_ROWS))),
        ],
        axis=0,
    )
    first, second = normalize(layer_input, gain)

    weight = lax.all_gather(packed, "fsdp", axis=0)

    own = swap_dp(jnp.broadcast_to(passage_rows[None], (RING, 64, 256))).reshape(RING * 64, 256)
    own = after(own, first, second)
    other = to_sibling(own)
    from_below = lax.ppermute(after(first, own), "dp", UPWARD)
    from_above = lax.ppermute(after(second, own), "dp", DOWNWARD)

    partial = pl.pallas_call(
        partial_scores_kernel,
        name="partial_scores",
        out_shape=jax.ShapeDtypeStruct((N_FSDP, 72, 256), F32),
        compiler_params=params(),
        cost_estimate=cost(2 * 64 * 256 * 2048 * 2, 2e6),
    )(query_rows, own, other)
    scores = pl.pallas_call(
        finish_scores_kernel,
        name="finish_scores",
        out_shape=jax.ShapeDtypeStruct((N_FSDP, 72, 256), F32),
        compiler_params=params(),
        cost_estimate=cost(64 * 256 * 20, 1.2e6),
    )(swap_fsdp(partial))
    scores = swap_fsdp(scores)
    owner = positive // 64
    place = (
        jnp.where(owner % 2 == core, 0, RING * 64) + (owner // 2) * 64 + positive % 64
    ).astype(jnp.int32)
    query_grad, pulls, columns_sum, rerun = pl.pallas_call(
        query_grad_kernel,
        name="query_grad",
        out_shape=[
            jax.ShapeDtypeStruct((64, 256), F32),
            jax.ShapeDtypeStruct((N_FSDP, 64, 256), F32),
            jax.ShapeDtypeStruct((N_FSDP, 8, 256), F32),
            jax.ShapeDtypeStruct((N_FSDP, 2, 256), F32),
        ],
        compiler_params=params(),
        cost_estimate=cost(2 * 128 * 256 * 2048, 2e6),
    )(scores, query_rows, place.reshape(64, 1), own, other)
    g = swap_fsdp(rerun)

    keep, give = pl.pallas_call(
        passage_terms_kernel,
        name="passage_terms",
        out_shape=[jax.ShapeDtypeStruct((RING * 64, 256), F32)] * 2,
        compiler_params=params(),
        cost_estimate=cost(2 * 128 * 256 * 2048, 6e6),
    )(pulls, columns_sum, query_rows, own, other)
    received = to_sibling(give)

    tokens = [first, second, to_sibling(first), to_sibling(second)]
    tokens += [from_below, from_above, to_sibling(from_below), to_sibling(from_above)]
    weight = after(weight, keep)
    *saved, = project(scalars, tokens, weight, cos, sin)
    g = after(g, saved[0])

    sent = (keep + received).astype(BF16).reshape(RING, 64, 256)
    arrived = swap_dp(sent)
    passage_grad = jnp.sum(arrived.astype(F32), axis=0)

    g = jnp.swapaxes(g, 0, 1)
    below, above = lax.ppermute(g[0:1], "dp", UPWARD), lax.ppermute(g[1:2], "dp", DOWNWARD)
    queries, keys = after(saved[0], g, sent), saved[1]
    weights, sums = attend(queries, keys)
    below = after(below, weights)
    g_own = jnp.concatenate([g, below, above], axis=0)
    g_other = to_sibling(g_own)
    grads = backward(
        scalars, tokens, g_own, g_other, [queries, keys, saved[2], weights, sums, *saved[3:]], cos, sin
    )
    grads = after(grads, arrived)

    summed = grads[0] + to_sibling(grads[1])
    shared = pl.pallas_call(
        fold_kernel,
        name="fold_fsdp",
        out_shape=jax.ShapeDtypeStruct((RING, RING * 8, HD), BF16),
        compiler_params=params(),
    )(swap_fsdp(summed.reshape(N_FSDP, RING * 8, HD)))
    total, squares = pl.pallas_call(
        total_kernel,
        name="total_dp",
        out_shape=[
            jax.ShapeDtypeStruct((RING * 8, HD), F32),
            jax.ShapeDtypeStruct((N_FSDP, 8, HD), F32),
        ],
        compiler_params=params(),
    )(swap_dp(shared))
    total_other = to_sibling(total)
    squares = swap_fsdp(squares)
    down, up = pl.pallas_call(
        finish_kernel,
        name="finish_clip",
        in_specs=[SMEM] + [VMEM] * 4,
        out_shape=[
            jax.ShapeDtypeStruct((LOW, ROWS), F32),
            jax.ShapeDtypeStruct((ADAPTER_RANK, UP_ROWS), F32),
        ],
        compiler_params=params(),
    )(scalars, total, total_other, squares, to_sibling(squares))
    return query_grad, passage_grad, down.T, up.T


def solution(mesh):
    in_specs = (
        P("dp", "fsdp"),
        P("dp", "fsdp"),
        P("dp"),
        P(("dp", "fsdp"), None, None),
        P(),
        P("fsdp", None),
        P("fsdp", None),
        P("fsdp", None),
    )
    out_specs = (P("dp", "fsdp"), P("dp", "fsdp"), P("fsdp", None), P("fsdp", None))
    return jax.shard_map(shards, mesh=mesh, in_specs=in_specs, out_specs=out_specs, check_vma=False)
```

```python
import functools
import math

import jax
import jax.numpy as jnp
import numpy as np
from jax import lax
from jax.experimental import pallas as pl
from jax.experimental.pallas import tpu as pltpu
from jax.sharding import PartitionSpec as P

MODEL_WIDTH = 4096
HD = 128
HQ = 16
HK = 4
GROUP = HQ // HK
ADAPTER_RANK = 16
L = 128
EPS_NORM = 1e-06
SOFTMAX_TEMPER = 0.02
ADAPTER_SCALE = 2.0
RMS_EPS = 1e-05
ROPE_BASE = 10000.0
MAX_NORM = 1.0

N_DP = 32
N_FSDP = 8
RING = N_DP // 2
ROWS = MODEL_WIDTH // N_FSDP
UP_ROWS = (HQ + 2 * HK) * HD // N_FSDP
COLS = (GROUP + 2) * HD
MAP = 2 * ADAPTER_RANK
LOW = 3 * ADAPTER_RANK
F32 = jnp.float32
BF16 = jnp.bfloat16
VMEM_LIMIT = 16 * 1024 * 1024
LARGE_VMEM = 40 * 1024 * 1024

NN = (((1,), (0,)), ((), ()))
NT = (((1,), (1,)), ((), ()))
TN = (((0,), (0,)), ((), ()))


def dot(a, b, dims=NN):
    return lax.dot_general(a, b, dims, preferred_element_type=F32)


def split(x):
    head = x.astype(BF16)
    return head, (x - head.astype(F32)).astype(BF16)


def params(limit=VMEM_LIMIT):
    return pltpu.CompilerParams(vmem_limit_bytes=limit)


def cost(flops, bytes_accessed):
    return pl.CostEstimate(flops=1, bytes_accessed=1, transcendentals=0)


VMEM = pl.BlockSpec(memory_space=pltpu.VMEM)
SMEM = pl.BlockSpec(memory_space=pltpu.SMEM)
ANY = pl.BlockSpec(memory_space=pl.ANY)


def rope_tables():
    half = HD // 2
    freqs = np.power(
        np.float32(ROPE_BASE), -(np.arange(half, dtype=np.float32) * np.float32(2.0)) / np.float32(HD)
    ).astype(np.float32)
    angles = np.arange(L, dtype=np.float32)[:, None] * freqs[None, :]
    cosine = np.cos(angles).astype(np.float32)
    sine = np.sin(angles).astype(np.float32)
    return np.concatenate([cosine, cosine], 1), np.concatenate([-sine, sine], 1)


def normalize_kernel(x_ref, gain_ref, first_ref, second_ref):
    for s, out_ref in enumerate((first_ref, second_ref)):
        values = x_ref[s].astype(F32)
        scale = lax.rsqrt(jnp.mean(values * values, axis=-1, keepdims=True) + RMS_EPS)
        out_ref[...] = (values * scale * gain_ref[...]).astype(BF16)


def normalize(x, gain):
    shape = jax.ShapeDtypeStruct((L, MODEL_WIDTH), BF16)
    step = 32
    return pl.pallas_call(
        normalize_kernel,
        name="normalize",
        grid=(L // step,),
        in_specs=[
            pl.BlockSpec((2, step, MODEL_WIDTH), lambda i: (0, i, 0)),
            pl.BlockSpec((1, MODEL_WIDTH), lambda i: (0, 0)),
        ],
        out_specs=[pl.BlockSpec((step, MODEL_WIDTH), lambda i: (i, 0))] * 2,
        out_shape=[shape, shape],
        compiler_params=params(),
        cost_estimate=cost(6 * 2 * L * MODEL_WIDTH, 8 * L * MODEL_WIDTH),
    )(x, gain.reshape(1, MODEL_WIDTH))


def eye_mask(n, m):
    return lax.broadcasted_iota(jnp.int32, (n, m), 0) == lax.broadcasted_iota(jnp.int32, (n, m), 1)


def column_of(row, n):
    return jnp.sum(jnp.where(eye_mask(n, row.shape[1]), row, 0.0), axis=1, keepdims=True)


def chunk_of(c, own_ref, other_ref, size=256):
    per = own_ref.shape[0] // size
    ref = own_ref if c < per else other_ref
    return ref[(c % per) * size : (c % per + 1) * size, :]


def partial_scores_kernel(q_ref, own_ref, other_ref, out_ref):
    q = q_ref[...]
    ones = jnp.ones((16, 256), BF16)
    rows = lax.broadcasted_iota(jnp.int32, (8, 256), 0)

    def square_row(block):
        values = block.astype(F32)
        head, rest = split(values * values)
        return (dot(ones, head, NT) + dot(ones, rest, NT))[0:8]

    q_row = square_row(jnp.concatenate([q, jnp.zeros((256 - 64, 256), BF16)], axis=0))
    for c in range(N_FSDP):
        passages = chunk_of(c, own_ref, other_ref)
        out_ref[c, 0:64, :] = dot(q, passages, NT)
        out_ref[c, 64:72, :] = jnp.where(
            rows == 0, square_row(passages), jnp.where(rows == 1, q_row, 0.0)
        )


def finish_scores_kernel(parts_ref, out_ref):
    total = parts_ref[0]
    for c in range(1, N_FSDP):
        total = total + parts_ref[c]
    p_norm = jnp.sqrt(total[64:65] + EPS_NORM)
    q_norm_row = jnp.sqrt(total[65:66] + EPS_NORM)
    q_norm = column_of(q_norm_row, 64)
    scores = total[0:64] / (q_norm * p_norm * SOFTMAX_TEMPER)
    rows = lax.broadcasted_iota(jnp.int32, (8, 256), 0)
    tail = jnp.where(rows == 0, p_norm, jnp.where(rows == 1, q_norm_row, 0.0))
    for c in range(N_FSDP):
        out_ref[c, 0:64, :] = scores
        out_ref[c, 64:72, :] = tail


def query_grad_kernel(s_ref, q_ref, pos_ref, own_ref, other_ref, grad_ref, w_ref, col_ref, rerun_ref):
    top = jnp.max(s_ref[0, 0:64, :], axis=1, keepdims=True)
    for c in range(1, N_FSDP):
        top = jnp.maximum(top, jnp.max(s_ref[c, 0:64, :], axis=1, keepdims=True))
    norm = jnp.zeros((64, 1), F32)
    for c in range(N_FSDP):
        norm = norm + jnp.sum(jnp.exp(s_ref[c, 0:64, :] - top), axis=1, keepdims=True)
    q_norm = column_of(s_ref[0, 65:66, :], 64)
    place = pos_ref[...]
    lane = lax.broadcasted_iota(jnp.int32, (64, 256), 1)
    cross = jnp.zeros((64, 1), F32)
    total = jnp.zeros((64, 256), F32)
    for c in range(N_FSDP):
        s = s_ref[c, 0:64, :]
        p_norm = s_ref[c, 64:65, :]
        grad = jnp.exp(s - top) / norm - jnp.where(lane + 256 * c == place, 1.0, 0.0)
        terms = grad * s
        cross = cross + jnp.sum(terms, axis=1, keepdims=True)
        column = jnp.sum(terms, axis=0, keepdims=True)
        col_ref[c] = jnp.broadcast_to(column / (p_norm * p_norm), (8, 256))
        weight = grad / (p_norm * SOFTMAX_TEMPER)
        w_ref[c] = weight / q_norm
        head, rest = split(weight)
        both = dot(jnp.concatenate([head, rest], axis=0), chunk_of(c, own_ref, other_ref))
        total = total + both[0:64] + both[64:128]
    query_grad = total / q_norm - (cross / (q_norm * q_norm)) * q_ref[...].astype(F32)
    grad_ref[...] = query_grad
    for m in range(N_FSDP):
        rerun_ref[m] = query_grad[2 * m : 2 * m + 2]


def passage_terms_kernel(scalar_ref, w_ref, col_ref, q_ref, own_ref, other_ref, keep_ref, give_ref):
    q = q_ref[...]
    twice = jnp.concatenate([q, q], axis=0)
    for c in range(N_FSDP):
        head, rest = split(w_ref[c])
        pulled = dot(jnp.concatenate([head, rest], axis=0), twice, TN)
        scale = column_of(col_ref[c, 0:1, :], 256)
        value = pulled - scale * chunk_of(c, own_ref, other_ref).astype(F32)
        out_ref = keep_ref if c < 4 else give_ref
        for b in range(4):
            place = (c % 4) * 256 + (b // 2) * 128 + (scalar_ref[2] + b % 2) % 2 * 64
            out_ref[pl.ds(pl.multiple_of(place, 64), 64), :] = value[64 * b : 64 * (b + 1)]


def project_kernel(
    scalar_ref, t0, t1, t2, t3, t4, t5, t6, t7, weight_ref, maps_ref, cos_ref, sin_ref,
    q_ref, k_ref, v_ref, low_ref, up_ref,
    tok, wv, maps, acc, lacc, tok_sem, w_sem,
):
    tokens = (t0, t1, t2, t3, t4, t5, t6, t7)
    head = scalar_ref[0]
    tok_copies = [
        pltpu.make_async_copy(t, tok.at[pl.ds(L * n, L)], tok_sem.at[n]) for n, t in enumerate(tokens)
    ]
    core = scalar_ref[1]
    w_copies = [
        pltpu.make_async_copy(weight_ref.at[n, pl.ds(0, ROWS)], wv.at[n], w_sem.at[n])
        for n in range(N_FSDP)
    ]
    map_copies = [
        pltpu.make_async_copy(weight_ref.at[:, pl.ds(ROWS, MAP)], maps.at[core], w_sem.at[N_FSDP]),
        pltpu.make_async_copy(maps_ref, maps.at[1 - core], w_sem.at[N_FSDP + 1]),
    ]
    for copy in tok_copies[:2] + w_copies[:2] + map_copies + w_copies[2:] + tok_copies[2:]:
        copy.start()

    cos = cos_ref[...]
    sin = sin_ref[...]
    def rope(x):
        return (x * cos + pltpu.roll(x, HD // 2, 1) * sin).astype(BF16)

    for copy in map_copies:
        copy.wait()
    up_ref[...] = jnp.zeros_like(up_ref)
    for j in range(GROUP + 2):
        tile = GROUP * head + j if j < GROUP else (HQ + HK * (j - GROUP)) + head
        lanes = pl.ds(pl.multiple_of((tile % 3) * HD, HD), HD)
        block = max(0, j - GROUP + 1)
        up_ref[ADAPTER_RANK * block : ADAPTER_RANK * (block + 1), HD * j : HD * (j + 1)] = (
            maps[1, tile // 3, ADAPTER_RANK : 2 * ADAPTER_RANK, lanes]
        )
    for i in range(4):
        tok_copies[2 * i].wait()
        tok_copies[2 * i + 1].wait()
        rows = slice(2 * L * i, 2 * L * (i + 1))
        for n in range(N_FSDP):
            if i == 0:
                w_copies[n].wait()
            x = tok[rows, ROWS * n : ROWS * (n + 1)]
            part = dot(x, wv[n])
            down = jnp.concatenate([maps[0, n, :, 0:ROWS], maps[1, n, 0:ADAPTER_RANK, 0:ROWS]], axis=0)
            low_part = dot(x, down, NT)
            total = part if n == 0 else total + part
            low_sum = low_part if n == 0 else low_sum + low_part

        low = low_sum.astype(BF16)
        acc[...] = total + ADAPTER_SCALE * dot(low, up_ref[...])
        for s in range(2):
            n = 2 * i + s
            r = slice(L * s, L * (s + 1))
            low_ref[n] = low[r]
            q_ref[n] = jnp.concatenate([rope(acc[r, HD * j : HD * (j + 1)]) for j in range(GROUP)], axis=0)
            k_ref[n] = rope(acc[r, GROUP * HD : (GROUP + 1) * HD])
            v_ref[n] = acc[r, (GROUP + 1) * HD : (GROUP + 2) * HD].astype(BF16)


def project(scalars, tokens, weight, maps, cos, sin):
    n = len(tokens)
    return pl.pallas_call(
        project_kernel,
        name="project",
        in_specs=[SMEM] + [ANY] * (n + 2) + [VMEM, VMEM],
        out_specs=[VMEM] * 5,
        out_shape=[
            jax.ShapeDtypeStruct((n, GROUP * L, HD), BF16),
            jax.ShapeDtypeStruct((n, L, HD), BF16),
            jax.ShapeDtypeStruct((n, L, HD), BF16),
            jax.ShapeDtypeStruct((n, L, LOW), BF16),
            jax.ShapeDtypeStruct((LOW, COLS), BF16),
        ],
        scratch_shapes=[
            pltpu.VMEM((n * L, MODEL_WIDTH), BF16),
            pltpu.VMEM((N_FSDP, ROWS, COLS), BF16),
            pltpu.VMEM((2, N_FSDP, MAP, COLS), BF16),
            pltpu.VMEM((2 * L, COLS), F32),
            pltpu.VMEM((2 * L, LOW), F32),
            pltpu.SemaphoreType.DMA((n,)),
            pltpu.SemaphoreType.DMA((N_FSDP + 2,)),
        ],
        compiler_params=params(LARGE_VMEM),
        cost_estimate=cost(2 * n * L * MODEL_WIDTH * (COLS + LOW), 20e6),
    )(scalars, *tokens, weight, maps, cos, sin)


def attend_kernel(q_ref, k_ref, p_ref, csum_ref):
    causal = lax.broadcasted_iota(jnp.int32, (L, L), 0) >= lax.broadcasted_iota(jnp.int32, (L, L), 1)
    causal = jnp.concatenate([causal.astype(F32)] * GROUP, axis=0) > 0.5

    @pl.loop(0, q_ref.shape[0], unroll=4)
    def _(n):
        scores = dot(q_ref[n], k_ref[n], NT) / math.sqrt(HD)
        scores = jnp.where(causal, scores, -1e30)
        e = jnp.exp(scores - jnp.max(scores, axis=1, keepdims=True))
        p = e / jnp.sum(e, axis=1, keepdims=True)
        p_ref[n] = p
        rounded = p.astype(BF16).astype(F32)
        csum_ref[n] = jnp.zeros((8, L), F32)
        for j in range(GROUP):
            csum_ref[n, j : j + 1, :] = jnp.sum(rounded[L * j : L * (j + 1)], axis=0, keepdims=True)


def attend(queries, keys):
    n = queries.shape[0]
    return pl.pallas_call(
        attend_kernel,
        name="attend",
        in_specs=[VMEM, VMEM],
        out_specs=[VMEM, VMEM],
        out_shape=[
            jax.ShapeDtypeStruct((n, GROUP * L, L), F32),
            jax.ShapeDtypeStruct((n, 8, L), F32),
        ],
        compiler_params=params(),
        cost_estimate=cost(2 * n * GROUP * L * L * HD * 10, 4e6),
    )(queries, keys)


def backward_kernel(
    scalar_ref, t0, t1, t2, t3, t4, t5, t6, t7, g_own, g_other, q_ref, k_ref, v_ref, p_ref,
    csum_ref, low_ref, up_ref, cos_ref, sin_ref, keep_ref, give_ref, tok, dlow, dup, g_all, sums, tok_sem,
):
    tokens = (t0, t1, t2, t3, t4, t5, t6, t7)
    head = scalar_ref[0]
    core = scalar_ref[1]
    copies = [
        pltpu.make_async_copy(t, tok.at[pl.ds(L * n, L)], tok_sem.at[n]) for n, t in enumerate(tokens)
    ]
    for copy in copies:
        copy.start()
    cos = cos_ref[...]
    sin = sin_ref[...]
    up = up_ref[...]
    g_all[...] = jnp.zeros_like(g_all)
    shard_row = lax.broadcasted_iota(jnp.int32, (N_FSDP, 256), 0)
    for n in range(8):
        ref = (g_own, g_other)[(n // 2) % 2]
        rows = ref[(n // 4) * 2 + n % 2] / L
        for j in range(2):
            row = jnp.sum(jnp.where(shard_row == 2 * head + j, rows, 0.0), axis=0, keepdims=True)
            g_all[n, 2 * j : 2 * j + 1, :] = row[:, 0:HD]
            g_all[n, 2 * j + 1 : 2 * j + 2, :] = row[:, HD : 2 * HD]
    dup[...] = jnp.zeros_like(dup)

    def unrope(x):
        return x * cos + pltpu.roll(x * sin, HD // 2, 1)

    @pl.loop(0, 8, unroll=4)
    def _(n):
        g = g_all[n]
        g_head, g_rest = split(g)
        v = v_ref[n]
        k = k_ref[n]
        q = q_ref[n]
        u = dot(jnp.concatenate([g_head, g_rest], axis=0), v, NT)
        u = u[0:8] + u[8:16]
        parts = []
        for j in range(GROUP):
            p = p_ref[n, L * j : L * (j + 1), :]
            pu = p * u[j : j + 1]
            parts.append((pu - p * jnp.sum(pu, axis=1, keepdims=True)) * (1.0 / math.sqrt(HD)))
        ds_head, ds_rest = split(jnp.concatenate(parts, axis=0))
        dq = dot(ds_head, k) + dot(ds_rest, k)
        dk = dot(ds_head, q, TN) + dot(ds_rest, q, TN)
        c_head, c_rest = split(csum_ref[n])
        dv = dot(
            jnp.concatenate([c_head, c_rest, c_head, c_rest], axis=0),
            jnp.concatenate([g_head, g_head, g_rest, g_rest], axis=0),
            TN,
        )
        dproj = jnp.concatenate(
            [unrope(dq[L * j : L * (j + 1)]) for j in range(GROUP)] + [unrope(dk), dv], axis=1
        )
        head_part, rest_part = split(ADAPTER_SCALE * dproj)
        low_grad = dot(up, head_part, NT) + dot(up, rest_part, NT)
        l_head, l_rest = split(low_grad)
        lanes = pl.ds(pl.multiple_of(n * L, L), L)
        dlow[0:LOW, lanes] = l_head
        dlow[LOW : 2 * LOW, lanes] = l_rest
        low = low_ref[n]
        dup[...] += dot(low, head_part, TN) + dot(low, rest_part, TN)

    sums[1, :, RING // 2 : RING] = jnp.zeros((N_FSDP, RING // 2, 8, HD), F32)
    for j in range(GROUP + 2):
        tile = GROUP * head + j if j < GROUP else (HQ + HK * (j - GROUP)) + head
        shard = tile // 3
        block = max(0, j - GROUP + 1)
        value = dup[ADAPTER_RANK * block : ADAPTER_RANK * (block + 1), HD * j : HD * (j + 1)]
        for i in range(2):
            sums[1, shard, RING // 2 + 2 * (tile % 3) + i] = value[8 * i : 8 * (i + 1)]
    for copy in copies:
        copy.wait()
    for f in range(N_FSDP):
        both = dot(dlow[...], tok[:, ROWS * f : ROWS * (f + 1)])
        value = both[0:LOW] + both[LOW : 2 * LOW]
        for b in range(ROWS // HD):
            for i in range(LOW // 8):
                group = b * (LOW // 8) + i
                sums[group // RING, f, group % RING] = value[8 * i : 8 * (i + 1), HD * b : HD * (b + 1)]
    keep_ref[...] = sums[core]
    give_ref[...] = sums[1 - core]


def backward(scalars, tokens, g_own, g_other, saved, cos, sin):
    n = len(tokens)
    return pl.pallas_call(
        backward_kernel,
        name="attention_backward",
        in_specs=[SMEM] + [ANY] * n + [VMEM] * 11,
        out_specs=[VMEM, VMEM],
        out_shape=[jax.ShapeDtypeStruct((N_FSDP, RING, 8, HD), F32)] * 2,
        scratch_shapes=[
            pltpu.VMEM((n * L, MODEL_WIDTH), BF16),
            pltpu.VMEM((2 * LOW, n * L), BF16),
            pltpu.VMEM((LOW, COLS), F32),
            pltpu.VMEM((n, 8, HD), F32),
            pltpu.VMEM((2, N_FSDP, RING, 8, HD), F32),
            pltpu.SemaphoreType.DMA((n,)),
        ],
        compiler_params=params(LARGE_VMEM),
        cost_estimate=cost(2 * n * L * MODEL_WIDTH * 2 * LOW, 15e6),
    )(scalars, *tokens, g_own, g_other, *saved, cos, sin)


def fold_kernel(parts_ref, out_ref):
    total = parts_ref[0]
    for n in range(1, N_FSDP):
        total = total + parts_ref[n]
    total = total.astype(BF16)
    for n in range(RING):
        out_ref[n] = total


def total_kernel(parts_ref, out_ref, squares_ref):
    total = parts_ref[0].astype(F32)
    for n in range(1, RING):
        total = total + parts_ref[n].astype(F32)
    out_ref[...] = total
    squares = jnp.broadcast_to(jnp.sum(total * total, axis=0, keepdims=True), (8, HD))
    for n in range(N_FSDP):
        squares_ref[n] = squares


def finish_kernel(scalar_ref, own_ref, other_ref, squares_ref, squares_other_ref, down_ref, up_ref):
    core = scalar_ref[1]
    squares = jnp.sum(squares_ref[:, 0:1, :], axis=0) + jnp.sum(squares_other_ref[:, 0:1, :], axis=0)
    grad_norm = jnp.sqrt(jnp.sum(squares, axis=1, keepdims=True))
    unit_scale = math.sqrt(3 * MODEL_WIDTH * ADAPTER_RANK + (HQ + 2 * HK) * HD * ADAPTER_RANK)
    factor = jnp.minimum(1.0, MAX_NORM / (grad_norm + 1e-06)) * unit_scale

    def tile(group):
        half, spot = divmod(group, RING)
        a = own_ref[8 * spot : 8 * spot + 8, :]
        b = other_ref[8 * spot : 8 * spot + 8, :]
        return jnp.where(core == half, a, b) * factor

    for b in range(ROWS // HD):
        for i in range(LOW // 8):
            down_ref[8 * i : 8 * (i + 1), HD * b : HD * (b + 1)] = tile(b * (LOW // 8) + i)
    for b in range(UP_ROWS // HD):
        for i in range(ADAPTER_RANK // 8):
            group = (ROWS // HD) * (LOW // 8) + 2 * b + i
            up_ref[8 * i : 8 * (i + 1), HD * b : HD * (b + 1)] = tile(group)


def dp_pairs(move):
    pairs = []
    for d in range(N_DP):
        z, y, core = move(d // 4, (d // 2) % 2, d % 2)
        pairs.append((d, (z % (N_DP // 4)) * 4 + y * 2 + core))
    return pairs


Y_PARTNER = dp_pairs(lambda z, y, c: (z, 1 - y, c))
Z_GROUPS = [[4 * z + i for z in range(N_DP // 4)] for i in range(4)]
SIBLING = dp_pairs(lambda z, y, c: (z, y, 1 - c))
UPWARD = dp_pairs(lambda z, y, c: (z + 1, y, c))
DOWNWARD = dp_pairs(lambda z, y, c: (z - 1, y, c))
CORE_GROUPS = [[2 * i + c for i in range(RING)] for c in range(2)]


def to_sibling(x):
    return lax.ppermute(x, "dp", SIBLING)


def after(x, *others):
    return lax.optimization_barrier((x,) + others)[0]


def swap_dp(x):
    return lax.all_to_all(x, "dp", 0, 0, axis_index_groups=CORE_GROUPS)


def swap_fsdp(x):
    return lax.all_to_all(x, "fsdp", 0, 0)


def shards(
    query_rows, passage_rows, positive, layer_input, gain, frozen_weight, down_maps, up_maps
):
    dp = lax.axis_index("dp")
    core = dp % 2
    head = 2 * ((dp // 4) % 2) + core
    y_hi = (dp // 2) % 2
    cos, sin = (jnp.asarray(t) for t in rope_tables())

    scalars = jnp.stack([head, core, y_hi]).astype(jnp.int32)
    columns = [
        lax.dynamic_slice_in_dim(frozen_weight, GROUP * HD * head, GROUP * HD, 1),
        lax.dynamic_slice_in_dim(frozen_weight, HQ * HD + HD * head, HD, 1),
        lax.dynamic_slice_in_dim(frozen_weight, (HQ + HK) * HD + HD * head, HD, 1),
    ]
    maps = jnp.stack(
        [
            jnp.pad(down_maps.T[:MAP], ((0, 0), (0, COLS - ROWS))),
            jnp.concatenate(
                [
                    jnp.pad(down_maps.T[MAP:], ((0, 0), (0, COLS - ROWS))),
                    jnp.pad(up_maps.T, ((0, 0), (0, COLS - UP_ROWS))),
                ],
                axis=0,
            ),
        ]
    )
    mine = lax.dynamic_index_in_dim(maps, core, 0, keepdims=False)
    packed = jnp.concatenate([jnp.concatenate(columns, axis=1), mine], axis=0)
    weight = lax.all_gather(packed, "fsdp", axis=0)
    first, second = normalize(layer_input, gain)

    pair = jnp.stack([passage_rows, lax.ppermute(passage_rows, "dp", Y_PARTNER)])
    own = lax.all_to_all(
        jnp.broadcast_to(pair[None], (N_DP // 4, 2, 64, 256)), "dp", 0, 0, axis_index_groups=Z_GROUPS
    ).reshape(RING * 64, 256)
    own = after(own, first, second)
    other = to_sibling(own)
    from_below = lax.ppermute(after(first, own), "dp", UPWARD)
    from_above = lax.ppermute(after(second, own), "dp", DOWNWARD)

    partial = pl.pallas_call(
        partial_scores_kernel,
        name="partial_scores",
        out_shape=jax.ShapeDtypeStruct((N_FSDP, 72, 256), F32),
        compiler_params=params(),
        cost_estimate=cost(2 * 64 * 256 * 2048 * 2, 2e6),
    )(query_rows, own, other)
    scores = pl.pallas_call(
        finish_scores_kernel,
        name="finish_scores",
        out_shape=jax.ShapeDtypeStruct((N_FSDP, 72, 256), F32),
        compiler_params=params(),
        cost_estimate=cost(64 * 256 * 20, 1.2e6),
    )(swap_fsdp(partial))
    scores = after(swap_fsdp(scores), from_below, from_above)
    owner = positive // 64
    place = (
        jnp.where(owner % 2 == core, 0, RING * 64)
        + (owner // 4) * 128
        + jnp.where((owner // 2) % 2 == y_hi, 0, 64)
        + positive % 64
    ).astype(jnp.int32)
    query_grad, pulls, columns_sum, rerun = pl.pallas_call(
        query_grad_kernel,
        name="query_grad",
        out_shape=[
            jax.ShapeDtypeStruct((64, 256), F32),
            jax.ShapeDtypeStruct((N_FSDP, 64, 256), F32),
            jax.ShapeDtypeStruct((N_FSDP, 8, 256), F32),
            jax.ShapeDtypeStruct((N_FSDP, 2, 256), F32),
        ],
        compiler_params=params(),
        cost_estimate=cost(2 * 128 * 256 * 2048, 2e6),
    )(scores, query_rows, place.reshape(64, 1), own, other)
    g = swap_fsdp(rerun)

    keep, give = pl.pallas_call(
        passage_terms_kernel,
        name="passage_terms",
        in_specs=[SMEM] + [VMEM] * 5,
        out_shape=[jax.ShapeDtypeStruct((RING * 64, 256), F32)] * 2,
        compiler_params=params(),
        cost_estimate=cost(2 * 128 * 256 * 2048, 6e6),
    )(scalars, after(pulls, g), columns_sum, query_rows, own, other)
    received = to_sibling(give)

    tokens = [first, second, to_sibling(first), to_sibling(second)]
    tokens += [from_below, from_above, to_sibling(from_below), to_sibling(from_above)]
    sent = (keep + received).astype(BF16).reshape(RING, 64, 256)
    arrived = swap_dp(sent)
    passage_grad = jnp.sum(arrived.astype(F32), axis=0)

    g = jnp.swapaxes(g, 0, 1)
    below, above = lax.ppermute(g[0:1], "dp", UPWARD), lax.ppermute(g[1:2], "dp", DOWNWARD)
    weight = after(weight, sent)
    maps_other = to_sibling(weight[:, ROWS:])
    *saved, = project(scalars, tokens, weight, maps_other, cos, sin)
    queries, keys = saved[:2]
    weights, sums = attend(queries, keys)
    below = after(below, queries)
    g_own = jnp.concatenate([g, below, above], axis=0)
    g_other = to_sibling(g_own)
    kept, given = backward(
        scalars, tokens, g_own, g_other, [queries, keys, saved[2], weights, sums, *saved[3:]], cos, sin
    )
    given = after(given, arrived)

    summed = kept + to_sibling(given)
    shared = pl.pallas_call(
        fold_kernel,
        name="fold_fsdp",
        out_shape=jax.ShapeDtypeStruct((RING, RING * 8, HD), BF16),
        compiler_params=params(),
    )(swap_fsdp(summed.reshape(N_FSDP, RING * 8, HD)))
    total, squares = pl.pallas_call(
        total_kernel,
        name="total_dp",
        out_shape=[
            jax.ShapeDtypeStruct((RING * 8, HD), F32),
            jax.ShapeDtypeStruct((N_FSDP, 8, HD), F32),
        ],
        compiler_params=params(),
    )(swap_dp(shared))
    total_other = to_sibling(total)
    squares = swap_fsdp(squares)
    down, up = pl.pallas_call(
        finish_kernel,
        name="finish_clip",
        in_specs=[SMEM] + [VMEM] * 4,
        out_shape=[
            jax.ShapeDtypeStruct((LOW, ROWS), F32),
            jax.ShapeDtypeStruct((ADAPTER_RANK, UP_ROWS), F32),
        ],
        compiler_params=params(),
    )(scalars, total, total_other, squares, to_sibling(after(squares, passage_grad)))
    return query_grad, passage_grad, down.T, up.T


def solution(mesh):
    in_specs = (
        P("dp", "fsdp"),
        P("dp", "fsdp"),
        P("dp"),
        P(("dp", "fsdp"), None, None),
        P(),
        P("fsdp", None),
        P("fsdp", None),
        P("fsdp", None),
    )
    out_specs = (P("dp", "fsdp"), P("dp", "fsdp"), P("fsdp", None), P("fsdp", None))
    return jax.shard_map(shards, mesh=mesh, in_specs=in_specs, out_specs=out_specs, check_vma=False)
```

```python
import functools
import math

import jax
import jax.numpy as jnp
import numpy as np
from jax import lax
from jax.experimental import pallas as pl
from jax.experimental.pallas import tpu as pltpu
from jax.sharding import PartitionSpec as P

MODEL_WIDTH = 4096
HD = 128
HQ = 16
HK = 4
GROUP = HQ // HK
ADAPTER_RANK = 16
L = 128
EPS_NORM = 1e-06
SOFTMAX_TEMPER = 0.02
ADAPTER_SCALE = 2.0
RMS_EPS = 1e-05
ROPE_BASE = 10000.0
MAX_NORM = 1.0

N_DP = 32
N_FSDP = 8
RING = N_DP // 2
ROWS = MODEL_WIDTH // N_FSDP
UP_ROWS = (HQ + 2 * HK) * HD // N_FSDP
COLS = (GROUP + 2) * HD
MAP = 2 * ADAPTER_RANK
LOW = 3 * ADAPTER_RANK
F32 = jnp.float32
BF16 = jnp.bfloat16
VMEM_LIMIT = 16 * 1024 * 1024
LARGE_VMEM = 40 * 1024 * 1024

NN = (((1,), (0,)), ((), ()))
NT = (((1,), (1,)), ((), ()))
TN = (((0,), (0,)), ((), ()))


def dot(a, b, dims=NN):
    return lax.dot_general(a, b, dims, preferred_element_type=F32)


def split(x):
    head = x.astype(BF16)
    return head, (x - head.astype(F32)).astype(BF16)


def params(limit=VMEM_LIMIT):
    return pltpu.CompilerParams(vmem_limit_bytes=limit)


def cost(flops, bytes_accessed):
    return pl.CostEstimate(flops=1, bytes_accessed=1, transcendentals=0)


VMEM = pl.BlockSpec(memory_space=pltpu.VMEM)
SMEM = pl.BlockSpec(memory_space=pltpu.SMEM)
ANY = pl.BlockSpec(memory_space=pl.ANY)


def rope_tables():
    half = HD // 2
    freqs = np.power(
        np.float32(ROPE_BASE), -(np.arange(half, dtype=np.float32) * np.float32(2.0)) / np.float32(HD)
    ).astype(np.float32)
    angles = np.arange(L, dtype=np.float32)[:, None] * freqs[None, :]
    cosine = np.cos(angles).astype(np.float32)
    sine = np.sin(angles).astype(np.float32)
    return np.concatenate([cosine, cosine], 1), np.concatenate([-sine, sine], 1)


def normalize_kernel(x_ref, gain_ref, first_ref, second_ref):
    for s, out_ref in enumerate((first_ref, second_ref)):
        values = x_ref[s].astype(F32)
        scale = lax.rsqrt(jnp.mean(values * values, axis=-1, keepdims=True) + RMS_EPS)
        out_ref[...] = (values * scale * gain_ref[...]).astype(BF16)


def normalize(x, gain):
    shape = jax.ShapeDtypeStruct((L, MODEL_WIDTH), BF16)
    step = 32
    return pl.pallas_call(
        normalize_kernel,
        name="normalize",
        grid=(L // step,),
        in_specs=[
            pl.BlockSpec((2, step, MODEL_WIDTH), lambda i: (0, i, 0)),
            pl.BlockSpec((1, MODEL_WIDTH), lambda i: (0, 0)),
        ],
        out_specs=[pl.BlockSpec((step, MODEL_WIDTH), lambda i: (i, 0))] * 2,
        out_shape=[shape, shape],
        compiler_params=params(),
        cost_estimate=cost(6 * 2 * L * MODEL_WIDTH, 8 * L * MODEL_WIDTH),
    )(x, gain.reshape(1, MODEL_WIDTH))


def eye_mask(n, m):
    return lax.broadcasted_iota(jnp.int32, (n, m), 0) == lax.broadcasted_iota(jnp.int32, (n, m), 1)


def column_of(row, n):
    return jnp.sum(jnp.where(eye_mask(n, row.shape[1]), row, 0.0), axis=1, keepdims=True)


def chunk_of(c, own_ref, other_ref, size=256):
    per = own_ref.shape[0] // size
    ref = own_ref if c < per else other_ref
    return ref[(c % per) * size : (c % per + 1) * size, :]


def partial_scores_kernel(q_ref, own_ref, other_ref, out_ref):
    q = q_ref[...]
    ones = jnp.ones((16, 256), BF16)
    rows = lax.broadcasted_iota(jnp.int32, (8, 256), 0)

    def square_row(block):
        values = block.astype(F32)
        head, rest = split(values * values)
        return (dot(ones, head, NT) + dot(ones, rest, NT))[0:8]

    q_row = square_row(jnp.concatenate([q, jnp.zeros((256 - 64, 256), BF16)], axis=0))
    for c in range(N_FSDP):
        passages = chunk_of(c, own_ref, other_ref)
        out_ref[c, 0:64, :] = dot(q, passages, NT)
        out_ref[c, 64:72, :] = jnp.where(
            rows == 0, square_row(passages), jnp.where(rows == 1, q_row, 0.0)
        )


def finish_scores_kernel(parts_ref, out_ref):
    total = parts_ref[0]
    for c in range(1, N_FSDP):
        total = total + parts_ref[c]
    p_norm = jnp.sqrt(total[64:65] + EPS_NORM)
    q_norm_row = jnp.sqrt(total[65:66] + EPS_NORM)
    q_norm = column_of(q_norm_row, 64)
    scores = total[0:64] / (q_norm * p_norm * SOFTMAX_TEMPER)
    rows = lax.broadcasted_iota(jnp.int32, (8, 256), 0)
    tail = jnp.where(rows == 0, p_norm, jnp.where(rows == 1, q_norm_row, 0.0))
    for c in range(N_FSDP):
        out_ref[c, 0:64, :] = scores
        out_ref[c, 64:72, :] = tail


def query_grad_kernel(s_ref, q_ref, pos_ref, own_ref, other_ref, grad_ref, w_ref, col_ref, rerun_ref):
    top = jnp.max(s_ref[0, 0:64, :], axis=1, keepdims=True)
    for c in range(1, N_FSDP):
        top = jnp.maximum(top, jnp.max(s_ref[c, 0:64, :], axis=1, keepdims=True))
    norm = jnp.zeros((64, 1), F32)
    for c in range(N_FSDP):
        norm = norm + jnp.sum(jnp.exp(s_ref[c, 0:64, :] - top), axis=1, keepdims=True)
    q_norm = column_of(s_ref[0, 65:66, :], 64)
    place = pos_ref[...]
    lane = lax.broadcasted_iota(jnp.int32, (64, 256), 1)
    cross = jnp.zeros((64, 1), F32)
    total = jnp.zeros((64, 256), F32)
    for c in range(N_FSDP):
        s = s_ref[c, 0:64, :]
        p_norm = s_ref[c, 64:65, :]
        grad = jnp.exp(s - top) / norm - jnp.where(lane + 256 * c == place, 1.0, 0.0)
        terms = grad * s
        cross = cross + jnp.sum(terms, axis=1, keepdims=True)
        column = jnp.sum(terms, axis=0, keepdims=True)
        col_ref[c] = jnp.broadcast_to(column / (p_norm * p_norm), (8, 256))
        weight = grad / (p_norm * SOFTMAX_TEMPER)
        w_ref[c] = weight / q_norm
        head, rest = split(weight)
        both = dot(jnp.concatenate([head, rest], axis=0), chunk_of(c, own_ref, other_ref))
        total = total + both[0:64] + both[64:128]
    query_grad = total / q_norm - (cross / (q_norm * q_norm)) * q_ref[...].astype(F32)
    grad_ref[...] = query_grad
    for m in range(N_FSDP):
        rerun_ref[m] = query_grad[2 * m : 2 * m + 2]


def passage_terms_kernel(scalar_ref, w_ref, col_ref, q_ref, own_ref, other_ref, keep_ref, give_ref):
    q = q_ref[...]
    twice = jnp.concatenate([q, q], axis=0)
    for c in range(N_FSDP):
        head, rest = split(w_ref[c])
        pulled = dot(jnp.concatenate([head, rest], axis=0), twice, TN)
        scale = column_of(col_ref[c, 0:1, :], 256)
        value = pulled - scale * chunk_of(c, own_ref, other_ref).astype(F32)
        out_ref = keep_ref if c < 4 else give_ref
        for b in range(4):
            place = (c % 4) * 256 + (b // 2) * 128 + (scalar_ref[2] + b % 2) % 2 * 64
            out_ref[pl.ds(pl.multiple_of(place, 64), 64), :] = value[64 * b : 64 * (b + 1)]


def project_kernel(
    scalar_ref, t0, t1, t2, t3, t4, t5, t6, t7, weight_ref, maps_ref, cos_ref, sin_ref,
    q_ref, k_ref, v_ref, low_ref, up_ref,
    tok, wv, maps, acc, lacc, tok_sem, w_sem,
):
    tokens = (t0, t1, t2, t3, t4, t5, t6, t7)
    head = scalar_ref[0]
    tok_copies = [
        pltpu.make_async_copy(t, tok.at[pl.ds(L * n, L)], tok_sem.at[n]) for n, t in enumerate(tokens)
    ]
    core = scalar_ref[1]
    w_copies = [
        pltpu.make_async_copy(weight_ref.at[n, pl.ds(0, ROWS)], wv.at[n], w_sem.at[n])
        for n in range(N_FSDP)
    ]
    map_copies = [
        pltpu.make_async_copy(weight_ref.at[:, pl.ds(ROWS, MAP)], maps.at[core], w_sem.at[N_FSDP]),
        pltpu.make_async_copy(maps_ref, maps.at[1 - core], w_sem.at[N_FSDP + 1]),
    ]
    for copy in tok_copies[:2] + w_copies[:2] + map_copies + w_copies[2:] + tok_copies[2:]:
        copy.start()

    cos = cos_ref[...]
    sin = sin_ref[...]
    def rope(x):
        return (x * cos + pltpu.roll(x, HD // 2, 1) * sin).astype(BF16)

    for copy in map_copies:
        copy.wait()
    up_ref[...] = jnp.zeros_like(up_ref)
    for j in range(GROUP + 2):
        tile = GROUP * head + j if j < GROUP else (HQ + HK * (j - GROUP)) + head
        lanes = pl.ds(pl.multiple_of((tile % 3) * HD, HD), HD)
        block = max(0, j - GROUP + 1)
        up_ref[ADAPTER_RANK * block : ADAPTER_RANK * (block + 1), HD * j : HD * (j + 1)] = (
            maps[1, tile // 3, ADAPTER_RANK : 2 * ADAPTER_RANK, lanes]
        )
    for i in range(4):
        tok_copies[2 * i].wait()
        tok_copies[2 * i + 1].wait()
        rows = slice(2 * L * i, 2 * L * (i + 1))
        for n in range(N_FSDP):
            if i == 0:
                w_copies[n].wait()
            x = tok[rows, ROWS * n : ROWS * (n + 1)]
            part = dot(x, wv[n])
            down = jnp.concatenate([maps[0, n, :, 0:ROWS], maps[1, n, 0:ADAPTER_RANK, 0:ROWS]], axis=0)
            low_part = dot(x, down, NT)
            total = part if n == 0 else total + part
            low_sum = low_part if n == 0 else low_sum + low_part

        low = low_sum.astype(BF16)
        acc[...] = total + ADAPTER_SCALE * dot(low, up_ref[...])
        for s in range(2):
            n = 2 * i + s
            r = slice(L * s, L * (s + 1))
            low_ref[n] = low[r]
            q_ref[n] = jnp.concatenate([rope(acc[r, HD * j : HD * (j + 1)]) for j in range(GROUP)], axis=0)
            k_ref[n] = rope(acc[r, GROUP * HD : (GROUP + 1) * HD])
            v_ref[n] = acc[r, (GROUP + 1) * HD : (GROUP + 2) * HD].astype(BF16)


def project(scalars, tokens, weight, maps, cos, sin):
    n = len(tokens)
    return pl.pallas_call(
        project_kernel,
        name="project",
        in_specs=[SMEM] + [ANY] * (n + 2) + [VMEM, VMEM],
        out_specs=[VMEM] * 5,
        out_shape=[
            jax.ShapeDtypeStruct((n, GROUP * L, HD), BF16),
            jax.ShapeDtypeStruct((n, L, HD), BF16),
            jax.ShapeDtypeStruct((n, L, HD), BF16),
            jax.ShapeDtypeStruct((n, L, LOW), BF16),
            jax.ShapeDtypeStruct((LOW, COLS), BF16),
        ],
        scratch_shapes=[
            pltpu.VMEM((n * L, MODEL_WIDTH), BF16),
            pltpu.VMEM((N_FSDP, ROWS, COLS), BF16),
            pltpu.VMEM((2, N_FSDP, MAP, COLS), BF16),
            pltpu.VMEM((2 * L, COLS), F32),
            pltpu.VMEM((2 * L, LOW), F32),
            pltpu.SemaphoreType.DMA((n,)),
            pltpu.SemaphoreType.DMA((N_FSDP + 2,)),
        ],
        compiler_params=params(LARGE_VMEM),
        cost_estimate=cost(2 * n * L * MODEL_WIDTH * (COLS + LOW), 20e6),
    )(scalars, *tokens, weight, maps, cos, sin)


def attend_kernel(q_ref, k_ref, p_ref, csum_ref):
    causal = lax.broadcasted_iota(jnp.int32, (L, L), 0) >= lax.broadcasted_iota(jnp.int32, (L, L), 1)
    causal = jnp.concatenate([causal.astype(F32)] * GROUP, axis=0) > 0.5

    @pl.loop(0, q_ref.shape[0], unroll=4)
    def _(n):
        scores = dot(q_ref[n], k_ref[n], NT) / math.sqrt(HD)
        scores = jnp.where(causal, scores, -1e30)
        e = jnp.exp(scores - jnp.max(scores, axis=1, keepdims=True))
        p = e / jnp.sum(e, axis=1, keepdims=True)
        p_ref[n] = p
        rounded = p.astype(BF16).astype(F32)
        csum_ref[n] = jnp.zeros((8, L), F32)
        for j in range(GROUP):
            csum_ref[n, j : j + 1, :] = jnp.sum(rounded[L * j : L * (j + 1)], axis=0, keepdims=True)


def attend(queries, keys):
    n = queries.shape[0]
    return pl.pallas_call(
        attend_kernel,
        name="attend",
        in_specs=[VMEM, VMEM],
        out_specs=[VMEM, VMEM],
        out_shape=[
            jax.ShapeDtypeStruct((n, GROUP * L, L), F32),
            jax.ShapeDtypeStruct((n, 8, L), F32),
        ],
        compiler_params=params(),
        cost_estimate=cost(2 * n * GROUP * L * L * HD * 10, 4e6),
    )(queries, keys)


def backward_kernel(
    scalar_ref, t0, t1, t2, t3, t4, t5, t6, t7, g_own, g_other, q_ref, k_ref, v_ref, p_ref,
    csum_ref, low_ref, up_ref, cos_ref, sin_ref, keep_ref, give_ref, tok, dlow, dup, g_all, sums, tok_sem,
):
    tokens = (t0, t1, t2, t3, t4, t5, t6, t7)
    head = scalar_ref[0]
    core = scalar_ref[1]
    copies = [
        pltpu.make_async_copy(t, tok.at[pl.ds(L * n, L)], tok_sem.at[n]) for n, t in enumerate(tokens)
    ]
    for copy in copies:
        copy.start()
    cos = cos_ref[...]
    sin = sin_ref[...]
    up = up_ref[...]
    g_all[...] = jnp.zeros_like(g_all)
    shard_row = lax.broadcasted_iota(jnp.int32, (N_FSDP, 256), 0)
    for n in range(8):
        ref = (g_own, g_other)[(n // 2) % 2]
        rows = ref[(n // 4) * 2 + n % 2] / L
        for j in range(2):
            row = jnp.sum(jnp.where(shard_row == 2 * head + j, rows, 0.0), axis=0, keepdims=True)
            g_all[n, 2 * j : 2 * j + 1, :] = row[:, 0:HD]
            g_all[n, 2 * j + 1 : 2 * j + 2, :] = row[:, HD : 2 * HD]
    dup[...] = jnp.zeros_like(dup)

    def unrope(x):
        return x * cos + pltpu.roll(x * sin, HD // 2, 1)

    @pl.loop(0, 8, unroll=4)
    def _(n):
        g = g_all[n]
        g_head, g_rest = split(g)
        v = v_ref[n]
        k = k_ref[n]
        q = q_ref[n]
        u = dot(jnp.concatenate([g_head, g_rest], axis=0), v, NT)
        u = u[0:8] + u[8:16]
        parts = []
        for j in range(GROUP):
            p = p_ref[n, L * j : L * (j + 1), :]
            pu = p * u[j : j + 1]
            parts.append((pu - p * jnp.sum(pu, axis=1, keepdims=True)) * (1.0 / math.sqrt(HD)))
        ds_head, ds_rest = split(jnp.concatenate(parts, axis=0))
        dq = dot(ds_head, k) + dot(ds_rest, k)
        dk = dot(ds_head, q, TN) + dot(ds_rest, q, TN)
        c_head, c_rest = split(csum_ref[n])
        dv = dot(
            jnp.concatenate([c_head, c_rest, c_head, c_rest], axis=0),
            jnp.concatenate([g_head, g_head, g_rest, g_rest], axis=0),
            TN,
        )
        dproj = jnp.concatenate(
            [unrope(dq[L * j : L * (j + 1)]) for j in range(GROUP)] + [unrope(dk), dv], axis=1
        )
        head_part, rest_part = split(ADAPTER_SCALE * dproj)
        low_grad = dot(up, head_part, NT) + dot(up, rest_part, NT)
        l_head, l_rest = split(low_grad)
        lanes = pl.ds(pl.multiple_of(n * L, L), L)
        dlow[0:LOW, lanes] = l_head
        dlow[LOW : 2 * LOW, lanes] = l_rest
        low = low_ref[n]
        dup[...] += dot(low, head_part, TN) + dot(low, rest_part, TN)

    sums[1, :, RING // 2 : RING] = jnp.zeros((N_FSDP, RING // 2, 8, HD), F32)
    for j in range(GROUP + 2):
        tile = GROUP * head + j if j < GROUP else (HQ + HK * (j - GROUP)) + head
        shard = tile // 3
        block = max(0, j - GROUP + 1)
        value = dup[ADAPTER_RANK * block : ADAPTER_RANK * (block + 1), HD * j : HD * (j + 1)]
        for i in range(2):
            sums[1, shard, RING // 2 + 2 * (tile % 3) + i] = value[8 * i : 8 * (i + 1)]
    for copy in copies:
        copy.wait()
    for f in range(N_FSDP):
        both = dot(dlow[...], tok[:, ROWS * f : ROWS * (f + 1)])
        value = both[0:LOW] + both[LOW : 2 * LOW]
        for b in range(ROWS // HD):
            for i in range(LOW // 8):
                group = b * (LOW // 8) + i
                sums[group // RING, f, group % RING] = value[8 * i : 8 * (i + 1), HD * b : HD * (b + 1)]
    keep_ref[...] = sums[core]
    give_ref[...] = sums[1 - core]


def backward(scalars, tokens, g_own, g_other, saved, cos, sin):
    n = len(tokens)
    return pl.pallas_call(
        backward_kernel,
        name="attention_backward",
        in_specs=[SMEM] + [ANY] * n + [VMEM] * 11,
        out_specs=[VMEM, VMEM],
        out_shape=[jax.ShapeDtypeStruct((N_FSDP, RING, 8, HD), F32)] * 2,
        scratch_shapes=[
            pltpu.VMEM((n * L, MODEL_WIDTH), BF16),
            pltpu.VMEM((2 * LOW, n * L), BF16),
            pltpu.VMEM((LOW, COLS), F32),
            pltpu.VMEM((n, 8, HD), F32),
            pltpu.VMEM((2, N_FSDP, RING, 8, HD), F32),
            pltpu.SemaphoreType.DMA((n,)),
        ],
        compiler_params=params(LARGE_VMEM),
        cost_estimate=cost(2 * n * L * MODEL_WIDTH * 2 * LOW, 15e6),
    )(scalars, *tokens, g_own, g_other, *saved, cos, sin)


def fold_kernel(parts_ref, out_ref):
    total = parts_ref[0]
    for n in range(1, N_FSDP):
        total = total + parts_ref[n]
    total = total.astype(BF16)
    for n in range(out_ref.shape[0]):
        out_ref[n] = total


def sum_kernel(parts_ref, out_ref):
    total = parts_ref[0].astype(F32)
    for n in range(1, parts_ref.shape[0]):
        total = total + parts_ref[n].astype(F32)
    out_ref[...] = total


def total_kernel(own_ref, other_ref, out_ref, squares_ref):
    total = own_ref[...] + other_ref[...]
    out_ref[...] = total
    squares = jnp.broadcast_to(jnp.sum(total * total, axis=0, keepdims=True), (8, HD))
    for n in range(N_FSDP):
        squares_ref[n] = squares


def finish_kernel(scalar_ref, own_ref, other_ref, squares_ref, squares_other_ref, down_ref, up_ref):
    core = scalar_ref[1]
    squares = jnp.sum(squares_ref[:, 0:1, :], axis=0) + jnp.sum(squares_other_ref[:, 0:1, :], axis=0)
    grad_norm = jnp.sqrt(jnp.sum(squares, axis=1, keepdims=True))
    unit_scale = math.sqrt(3 * MODEL_WIDTH * ADAPTER_RANK + (HQ + 2 * HK) * HD * ADAPTER_RANK)
    factor = jnp.minimum(1.0, MAX_NORM / (grad_norm + 1e-06)) * unit_scale

    def tile(group):
        half, spot = divmod(group, RING)
        a = own_ref[8 * spot : 8 * spot + 8, :]
        b = other_ref[8 * spot : 8 * spot + 8, :]
        return jnp.where(core == half, a, b) * factor

    for b in range(ROWS // HD):
        for i in range(LOW // 8):
            down_ref[8 * i : 8 * (i + 1), HD * b : HD * (b + 1)] = tile(b * (LOW // 8) + i)
    for b in range(UP_ROWS // HD):
        for i in range(ADAPTER_RANK // 8):
            group = (ROWS // HD) * (LOW // 8) + 2 * b + i
            up_ref[8 * i : 8 * (i + 1), HD * b : HD * (b + 1)] = tile(group)


def dp_pairs(move):
    pairs = []
    for d in range(N_DP):
        z, y, core = move(d // 4, (d // 2) % 2, d % 2)
        pairs.append((d, (z % (N_DP // 4)) * 4 + y * 2 + core))
    return pairs


Y_PARTNER = dp_pairs(lambda z, y, c: (z, 1 - y, c))
Z_GROUPS = [[4 * z + i for z in range(N_DP // 4)] for i in range(4)]
SIBLING = dp_pairs(lambda z, y, c: (z, y, 1 - c))
UPWARD = dp_pairs(lambda z, y, c: (z + 1, y, c))
DOWNWARD = dp_pairs(lambda z, y, c: (z - 1, y, c))
CORE_GROUPS = [[2 * i + c for i in range(RING)] for c in range(2)]


def to_sibling(x):
    return lax.ppermute(x, "dp", SIBLING)


def after(x, *others):
    return lax.optimization_barrier((x,) + others)[0]


def swap_dp(x):
    return lax.all_to_all(x, "dp", 0, 0, axis_index_groups=CORE_GROUPS)


def swap_z(x):
    return lax.all_to_all(x, "dp", 0, 0, axis_index_groups=Z_GROUPS)


def swap_fsdp(x):
    return lax.all_to_all(x, "fsdp", 0, 0)


def shards(
    query_rows, passage_rows, positive, layer_input, gain, frozen_weight, down_maps, up_maps
):
    dp = lax.axis_index("dp")
    core = dp % 2
    head = 2 * ((dp // 4) % 2) + core
    y_hi = (dp // 2) % 2
    cos, sin = (jnp.asarray(t) for t in rope_tables())

    scalars = jnp.stack([head, core, y_hi]).astype(jnp.int32)
    columns = [
        lax.dynamic_slice_in_dim(frozen_weight, GROUP * HD * head, GROUP * HD, 1),
        lax.dynamic_slice_in_dim(frozen_weight, HQ * HD + HD * head, HD, 1),
        lax.dynamic_slice_in_dim(frozen_weight, (HQ + HK) * HD + HD * head, HD, 1),
    ]
    maps = jnp.stack(
        [
            jnp.pad(down_maps.T[:MAP], ((0, 0), (0, COLS - ROWS))),
            jnp.concatenate(
                [
                    jnp.pad(down_maps.T[MAP:], ((0, 0), (0, COLS - ROWS))),
                    jnp.pad(up_maps.T, ((0, 0), (0, COLS - UP_ROWS))),
                ],
                axis=0,
            ),
        ]
    )
    mine = lax.dynamic_index_in_dim(maps, core, 0, keepdims=False)
    packed = jnp.concatenate([jnp.concatenate(columns, axis=1), mine], axis=0)
    weight = lax.all_gather(packed, "fsdp", axis=0)
    first, second = normalize(layer_input, gain)

    pair = jnp.stack([passage_rows, lax.ppermute(passage_rows, "dp", Y_PARTNER)])
    own = lax.all_to_all(
        jnp.broadcast_to(pair[None], (N_DP // 4, 2, 64, 256)), "dp", 0, 0, axis_index_groups=Z_GROUPS
    ).reshape(RING * 64, 256)
    own = after(own, first, second)
    other = to_sibling(own)
    from_below = lax.ppermute(after(first, own), "dp", UPWARD)
    from_above = lax.ppermute(after(second, own), "dp", DOWNWARD)

    partial = pl.pallas_call(
        partial_scores_kernel,
        name="partial_scores",
        out_shape=jax.ShapeDtypeStruct((N_FSDP, 72, 256), F32),
        compiler_params=params(),
        cost_estimate=cost(2 * 64 * 256 * 2048 * 2, 2e6),
    )(query_rows, own, other)
    scores = pl.pallas_call(
        finish_scores_kernel,
        name="finish_scores",
        out_shape=jax.ShapeDtypeStruct((N_FSDP, 72, 256), F32),
        compiler_params=params(),
        cost_estimate=cost(64 * 256 * 20, 1.2e6),
    )(swap_fsdp(partial))
    scores = after(swap_fsdp(scores), from_below, from_above)
    owner = positive // 64
    place = (
        jnp.where(owner % 2 == core, 0, RING * 64)
        + (owner // 4) * 128
        + jnp.where((owner // 2) % 2 == y_hi, 0, 64)
        + positive % 64
    ).astype(jnp.int32)
    query_grad, pulls, columns_sum, rerun = pl.pallas_call(
        query_grad_kernel,
        name="query_grad",
        out_shape=[
            jax.ShapeDtypeStruct((64, 256), F32),
            jax.ShapeDtypeStruct((N_FSDP, 64, 256), F32),
            jax.ShapeDtypeStruct((N_FSDP, 8, 256), F32),
            jax.ShapeDtypeStruct((N_FSDP, 2, 256), F32),
        ],
        compiler_params=params(),
        cost_estimate=cost(2 * 128 * 256 * 2048, 2e6),
    )(scores, query_rows, place.reshape(64, 1), own, other)
    g = swap_fsdp(rerun)

    keep, give = pl.pallas_call(
        passage_terms_kernel,
        name="passage_terms",
        in_specs=[SMEM] + [VMEM] * 5,
        out_shape=[jax.ShapeDtypeStruct((RING * 64, 256), F32)] * 2,
        compiler_params=params(),
        cost_estimate=cost(2 * 128 * 256 * 2048, 6e6),
    )(scalars, after(pulls, g), columns_sum, query_rows, own, other)
    received = to_sibling(give)

    tokens = [first, second, to_sibling(first), to_sibling(second)]
    tokens += [from_below, from_above, to_sibling(from_below), to_sibling(from_above)]
    sent = (keep + received).astype(BF16).reshape(RING, 64, 256)
    arrived = swap_dp(sent)
    passage_grad = jnp.sum(arrived.astype(F32), axis=0)

    g = jnp.swapaxes(g, 0, 1)
    below, above = lax.ppermute(g[0:1], "dp", UPWARD), lax.ppermute(g[1:2], "dp", DOWNWARD)
    weight = after(weight, sent)
    maps_other = to_sibling(weight[:, ROWS:])
    *saved, = project(scalars, tokens, weight, maps_other, cos, sin)
    queries, keys = saved[:2]
    weights, sums = attend(queries, keys)
    below = after(below, queries)
    g_own = jnp.concatenate([g, below, above], axis=0)
    g_other = to_sibling(g_own)
    kept, given = backward(
        scalars, tokens, g_own, g_other, [queries, keys, saved[2], weights, sums, *saved[3:]], cos, sin
    )
    given = after(given, arrived)

    summed = kept + to_sibling(given)
    shared = pl.pallas_call(
        fold_kernel,
        name="fold_fsdp",
        out_shape=jax.ShapeDtypeStruct((N_DP // 4, RING * 8, HD), BF16),
        compiler_params=params(),
    )(swap_fsdp(summed.reshape(N_FSDP, RING * 8, HD)))
    half = pl.pallas_call(
        sum_kernel,
        name="sum_z",
        out_shape=jax.ShapeDtypeStruct((RING * 8, HD), F32),
        compiler_params=params(),
    )(swap_z(shared))
    total, squares = pl.pallas_call(
        total_kernel,
        name="total_dp",
        out_shape=[
            jax.ShapeDtypeStruct((RING * 8, HD), F32),
            jax.ShapeDtypeStruct((N_FSDP, 8, HD), F32),
        ],
        compiler_params=params(),
    )(half, lax.ppermute(half, "dp", Y_PARTNER))
    total_other = to_sibling(total)
    squares = swap_fsdp(squares)
    down, up = pl.pallas_call(
        finish_kernel,
        name="finish_clip",
        in_specs=[SMEM] + [VMEM] * 4,
        out_shape=[
            jax.ShapeDtypeStruct((LOW, ROWS), F32),
            jax.ShapeDtypeStruct((ADAPTER_RANK, UP_ROWS), F32),
        ],
        compiler_params=params(),
    )(scalars, total, total_other, squares, to_sibling(after(squares, passage_grad)))
    return query_grad, passage_grad, down.T, up.T


def solution(mesh):
    in_specs = (
        P("dp", "fsdp"),
        P("dp", "fsdp"),
        P("dp"),
        P(("dp", "fsdp"), None, None),
        P(),
        P("fsdp", None),
        P("fsdp", None),
        P("fsdp", None),
    )
    out_specs = (P("dp", "fsdp"), P("dp", "fsdp"), P("fsdp", None), P("fsdp", None))
    return jax.shard_map(shards, mesh=mesh, in_specs=in_specs, out_specs=out_specs, check_vma=False)
```

```python
import functools
import math

import jax
import jax.numpy as jnp
import numpy as np
from jax import lax
from jax.experimental import pallas as pl
from jax.experimental.pallas import tpu as pltpu
from jax.sharding import PartitionSpec as P

MODEL_WIDTH = 4096
HD = 128
HQ = 16
HK = 4
GROUP = HQ // HK
ADAPTER_RANK = 16
L = 128
EPS_NORM = 1e-06
SOFTMAX_TEMPER = 0.02
ADAPTER_SCALE = 2.0
RMS_EPS = 1e-05
ROPE_BASE = 10000.0
MAX_NORM = 1.0

N_DP = 32
N_FSDP = 8
RING = N_DP // 2
ROWS = MODEL_WIDTH // N_FSDP
UP_ROWS = (HQ + 2 * HK) * HD // N_FSDP
COLS = (GROUP + 2) * HD
MAP = 2 * ADAPTER_RANK
LOW = 3 * ADAPTER_RANK
F32 = jnp.float32
BF16 = jnp.bfloat16
VMEM_LIMIT = 16 * 1024 * 1024
LARGE_VMEM = 40 * 1024 * 1024

NN = (((1,), (0,)), ((), ()))
NT = (((1,), (1,)), ((), ()))
TN = (((0,), (0,)), ((), ()))


def dot(a, b, dims=NN):
    return lax.dot_general(a, b, dims, preferred_element_type=F32)


def split(x):
    head = x.astype(BF16)
    return head, (x - head.astype(F32)).astype(BF16)


def params(limit=VMEM_LIMIT):
    return pltpu.CompilerParams(vmem_limit_bytes=limit)


def cost(flops, bytes_accessed):
    return pl.CostEstimate(flops=1, bytes_accessed=1, transcendentals=0)


VMEM = pl.BlockSpec(memory_space=pltpu.VMEM)
SMEM = pl.BlockSpec(memory_space=pltpu.SMEM)
ANY = pl.BlockSpec(memory_space=pl.ANY)


def rope_tables():
    half = HD // 2
    freqs = np.power(
        np.float32(ROPE_BASE), -(np.arange(half, dtype=np.float32) * np.float32(2.0)) / np.float32(HD)
    ).astype(np.float32)
    angles = np.arange(L, dtype=np.float32)[:, None] * freqs[None, :]
    cosine = np.cos(angles).astype(np.float32)
    sine = np.sin(angles).astype(np.float32)
    return np.concatenate([cosine, cosine], 1), np.concatenate([-sine, sine], 1)


def normalize_kernel(x_ref, gain_ref, first_ref, second_ref):
    for s, out_ref in enumerate((first_ref, second_ref)):
        values = x_ref[s].astype(F32)
        scale = lax.rsqrt(jnp.mean(values * values, axis=-1, keepdims=True) + RMS_EPS)
        out_ref[...] = (values * scale * gain_ref[...]).astype(BF16)


def normalize(x, gain):
    shape = jax.ShapeDtypeStruct((L, MODEL_WIDTH), BF16)
    step = 32
    return pl.pallas_call(
        normalize_kernel,
        name="normalize",
        grid=(L // step,),
        in_specs=[
            pl.BlockSpec((2, step, MODEL_WIDTH), lambda i: (0, i, 0)),
            pl.BlockSpec((1, MODEL_WIDTH), lambda i: (0, 0)),
        ],
        out_specs=[pl.BlockSpec((step, MODEL_WIDTH), lambda i: (i, 0))] * 2,
        out_shape=[shape, shape],
        compiler_params=params(),
        cost_estimate=cost(6 * 2 * L * MODEL_WIDTH, 8 * L * MODEL_WIDTH),
    )(x, gain.reshape(1, MODEL_WIDTH))


def eye_mask(n, m):
    return lax.broadcasted_iota(jnp.int32, (n, m), 0) == lax.broadcasted_iota(jnp.int32, (n, m), 1)


def column_of(row, n):
    return jnp.sum(jnp.where(eye_mask(n, row.shape[1]), row, 0.0), axis=1, keepdims=True)


def chunk_of(c, own_ref, other_ref, size=256):
    per = own_ref.shape[0] // size
    ref = own_ref if c < per else other_ref
    return ref[(c % per) * size : (c % per + 1) * size, :]


def partial_scores_kernel(q_ref, own_ref, other_ref, out_ref):
    q = q_ref[...]
    ones = jnp.ones((16, 256), BF16)
    rows = lax.broadcasted_iota(jnp.int32, (8, 256), 0)

    def square_row(block):
        values = block.astype(F32)
        head, rest = split(values * values)
        return (dot(ones, head, NT) + dot(ones, rest, NT))[0:8]

    q_row = square_row(jnp.concatenate([q, jnp.zeros((256 - 64, 256), BF16)], axis=0))
    for c in range(N_FSDP):
        passages = chunk_of(c, own_ref, other_ref)
        out_ref[c, 0:64, :] = dot(q, passages, NT)
        out_ref[c, 64:72, :] = jnp.where(
            rows == 0, square_row(passages), jnp.where(rows == 1, q_row, 0.0)
        )


def finish_scores_kernel(parts_ref, out_ref):
    total = parts_ref[0]
    for c in range(1, N_FSDP):
        total = total + parts_ref[c]
    p_norm = jnp.sqrt(total[64:65] + EPS_NORM)
    q_norm_row = jnp.sqrt(total[65:66] + EPS_NORM)
    q_norm = column_of(q_norm_row, 64)
    scores = total[0:64] / (q_norm * p_norm * SOFTMAX_TEMPER)
    rows = lax.broadcasted_iota(jnp.int32, (8, 256), 0)
    tail = jnp.where(rows == 0, p_norm, jnp.where(rows == 1, q_norm_row, 0.0))
    for c in range(N_FSDP):
        out_ref[c, 0:64, :] = scores
        out_ref[c, 64:72, :] = tail


def query_grad_kernel(s_ref, q_ref, pos_ref, own_ref, other_ref, grad_ref, w_ref, col_ref, rerun_ref):
    top = jnp.max(s_ref[0, 0:64, :], axis=1, keepdims=True)
    for c in range(1, N_FSDP):
        top = jnp.maximum(top, jnp.max(s_ref[c, 0:64, :], axis=1, keepdims=True))
    norm = jnp.zeros((64, 1), F32)
    for c in range(N_FSDP):
        norm = norm + jnp.sum(jnp.exp(s_ref[c, 0:64, :] - top), axis=1, keepdims=True)
    q_norm = column_of(s_ref[0, 65:66, :], 64)
    place = pos_ref[...]
    lane = lax.broadcasted_iota(jnp.int32, (64, 256), 1)
    cross = jnp.zeros((64, 1), F32)
    total = jnp.zeros((64, 256), F32)
    for c in range(N_FSDP):
        s = s_ref[c, 0:64, :]
        p_norm = s_ref[c, 64:65, :]
        grad = jnp.exp(s - top) / norm - jnp.where(lane + 256 * c == place, 1.0, 0.0)
        terms = grad * s
        cross = cross + jnp.sum(terms, axis=1, keepdims=True)
        column = jnp.sum(terms, axis=0, keepdims=True)
        col_ref[c] = jnp.broadcast_to(column / (p_norm * p_norm), (8, 256))
        weight = grad / (p_norm * SOFTMAX_TEMPER)
        w_ref[c] = weight / q_norm
        head, rest = split(weight)
        both = dot(jnp.concatenate([head, rest], axis=0), chunk_of(c, own_ref, other_ref))
        total = total + both[0:64] + both[64:128]
    query_grad = total / q_norm - (cross / (q_norm * q_norm)) * q_ref[...].astype(F32)
    grad_ref[...] = query_grad
    for m in range(N_FSDP):
        rerun_ref[m] = query_grad[2 * m : 2 * m + 2]


def passage_terms_kernel(w_ref, col_ref, q_ref, own_ref, other_ref, keep_ref, give_ref):
    q = q_ref[...]
    twice = jnp.concatenate([q, q], axis=0)
    for c in range(N_FSDP):
        head, rest = split(w_ref[c])
        pulled = dot(jnp.concatenate([head, rest], axis=0), twice, TN)
        scale = column_of(col_ref[c, 0:1, :], 256)
        value = pulled - scale * chunk_of(c, own_ref, other_ref).astype(F32)
        out_ref = keep_ref if c < 4 else give_ref
        out_ref[(c % 4) * 256 : (c % 4 + 1) * 256, :] = value


def project_kernel(
    scalar_ref, t0, t1, t2, t3, t4, t5, t6, t7, weight_ref, maps_ref, cos_ref, sin_ref,
    q_ref, k_ref, v_ref, low_ref, up_ref,
    tok, wv, maps, acc, lacc, tok_sem, w_sem,
):
    tokens = (t0, t1, t2, t3, t4, t5, t6, t7)
    head = scalar_ref[0]
    tok_copies = [
        pltpu.make_async_copy(t, tok.at[pl.ds(L * n, L)], tok_sem.at[n]) for n, t in enumerate(tokens)
    ]
    core = scalar_ref[1]
    w_copies = [
        pltpu.make_async_copy(weight_ref.at[n, pl.ds(0, ROWS)], wv.at[n], w_sem.at[n])
        for n in range(N_FSDP)
    ]
    map_copies = [
        pltpu.make_async_copy(weight_ref.at[:, pl.ds(ROWS, MAP)], maps.at[core], w_sem.at[N_FSDP]),
        pltpu.make_async_copy(maps_ref, maps.at[1 - core], w_sem.at[N_FSDP + 1]),
    ]
    for copy in tok_copies[:2] + w_copies[:2] + map_copies + w_copies[2:] + tok_copies[2:]:
        copy.start()

    cos = cos_ref[...]
    sin = sin_ref[...]
    def rope(x):
        return (x * cos + pltpu.roll(x, HD // 2, 1) * sin).astype(BF16)

    for copy in map_copies:
        copy.wait()
    up_ref[...] = jnp.zeros_like(up_ref)
    for j in range(GROUP + 2):
        tile = GROUP * head + j if j < GROUP else (HQ + HK * (j - GROUP)) + head
        lanes = pl.ds(pl.multiple_of((tile % 3) * HD, HD), HD)
        block = max(0, j - GROUP + 1)
        up_ref[ADAPTER_RANK * block : ADAPTER_RANK * (block + 1), HD * j : HD * (j + 1)] = (
            maps[1, tile // 3, ADAPTER_RANK : 2 * ADAPTER_RANK, lanes]
        )
    for i in range(4):
        tok_copies[2 * i].wait()
        tok_copies[2 * i + 1].wait()
        rows = slice(2 * L * i, 2 * L * (i + 1))
        for n in range(N_FSDP):
            if i == 0:
                w_copies[n].wait()
            x = tok[rows, ROWS * n : ROWS * (n + 1)]
            part = dot(x, wv[n])
            down = jnp.concatenate([maps[0, n, :, 0:ROWS], maps[1, n, 0:ADAPTER_RANK, 0:ROWS]], axis=0)
            low_part = dot(x, down, NT)
            total = part if n == 0 else total + part
            low_sum = low_part if n == 0 else low_sum + low_part

        low = low_sum.astype(BF16)
        acc[...] = total + ADAPTER_SCALE * dot(low, up_ref[...])
        for s in range(2):
            n = 2 * i + s
            r = slice(L * s, L * (s + 1))
            low_ref[n] = low[r]
            q_ref[n] = jnp.concatenate([rope(acc[r, HD * j : HD * (j + 1)]) for j in range(GROUP)], axis=0)
            k_ref[n] = rope(acc[r, GROUP * HD : (GROUP + 1) * HD])
            v_ref[n] = acc[r, (GROUP + 1) * HD : (GROUP + 2) * HD].astype(BF16)


def project(scalars, tokens, weight, maps, cos, sin):
    n = len(tokens)
    return pl.pallas_call(
        project_kernel,
        name="project",
        in_specs=[SMEM] + [ANY] * (n + 2) + [VMEM, VMEM],
        out_specs=[VMEM] * 5,
        out_shape=[
            jax.ShapeDtypeStruct((n, GROUP * L, HD), BF16),
            jax.ShapeDtypeStruct((n, L, HD), BF16),
            jax.ShapeDtypeStruct((n, L, HD), BF16),
            jax.ShapeDtypeStruct((n, L, LOW), BF16),
            jax.ShapeDtypeStruct((LOW, COLS), BF16),
        ],
        scratch_shapes=[
            pltpu.VMEM((n * L, MODEL_WIDTH), BF16),
            pltpu.VMEM((N_FSDP, ROWS, COLS), BF16),
            pltpu.VMEM((2, N_FSDP, MAP, COLS), BF16),
            pltpu.VMEM((2 * L, COLS), F32),
            pltpu.VMEM((2 * L, LOW), F32),
            pltpu.SemaphoreType.DMA((n,)),
            pltpu.SemaphoreType.DMA((N_FSDP + 2,)),
        ],
        compiler_params=params(LARGE_VMEM),
        cost_estimate=cost(2 * n * L * MODEL_WIDTH * (COLS + LOW), 20e6),
    )(scalars, *tokens, weight, maps, cos, sin)


def attend_kernel(q_ref, k_ref, p_ref, csum_ref):
    causal = lax.broadcasted_iota(jnp.int32, (L, L), 0) >= lax.broadcasted_iota(jnp.int32, (L, L), 1)
    causal = jnp.concatenate([causal.astype(F32)] * GROUP, axis=0) > 0.5

    @pl.loop(0, q_ref.shape[0], unroll=4)
    def _(n):
        scores = dot(q_ref[n], k_ref[n], NT) / math.sqrt(HD)
        scores = jnp.where(causal, scores, -1e30)
        e = jnp.exp(scores - jnp.max(scores, axis=1, keepdims=True))
        p = e / jnp.sum(e, axis=1, keepdims=True)
        p_ref[n] = p
        rounded = p.astype(BF16).astype(F32)
        csum_ref[n] = jnp.zeros((8, L), F32)
        for j in range(GROUP):
            csum_ref[n, j : j + 1, :] = jnp.sum(rounded[L * j : L * (j + 1)], axis=0, keepdims=True)


def attend(queries, keys):
    n = queries.shape[0]
    return pl.pallas_call(
        attend_kernel,
        name="attend",
        in_specs=[VMEM, VMEM],
        out_specs=[VMEM, VMEM],
        out_shape=[
            jax.ShapeDtypeStruct((n, GROUP * L, L), F32),
            jax.ShapeDtypeStruct((n, 8, L), F32),
        ],
        compiler_params=params(),
        cost_estimate=cost(2 * n * GROUP * L * L * HD * 10, 4e6),
    )(queries, keys)


def backward_kernel(
    scalar_ref, t0, t1, t2, t3, t4, t5, t6, t7, g_own, g_other, q_ref, k_ref, v_ref, p_ref,
    csum_ref, low_ref, up_ref, cos_ref, sin_ref, keep_ref, give_ref, tok, dlow, dup, g_all, sums, tok_sem,
):
    tokens = (t0, t1, t2, t3, t4, t5, t6, t7)
    head = scalar_ref[0]
    core = scalar_ref[1]
    copies = [
        pltpu.make_async_copy(t, tok.at[pl.ds(L * n, L)], tok_sem.at[n]) for n, t in enumerate(tokens)
    ]
    for copy in copies:
        copy.start()
    cos = cos_ref[...]
    sin = sin_ref[...]
    up = up_ref[...]
    g_all[...] = jnp.zeros_like(g_all)
    shard_row = lax.broadcasted_iota(jnp.int32, (N_FSDP, 256), 0)
    for n in range(8):
        ref = (g_own, g_other)[(n // 2) % 2]
        rows = ref[(n // 4) * 2 + n % 2] / L
        for j in range(2):
            row = jnp.sum(jnp.where(shard_row == 2 * head + j, rows, 0.0), axis=0, keepdims=True)
            g_all[n, 2 * j : 2 * j + 1, :] = row[:, 0:HD]
            g_all[n, 2 * j + 1 : 2 * j + 2, :] = row[:, HD : 2 * HD]
    dup[...] = jnp.zeros_like(dup)

    def unrope(x):
        return x * cos + pltpu.roll(x * sin, HD // 2, 1)

    @pl.loop(0, 8, unroll=4)
    def _(n):
        g = g_all[n]
        g_head, g_rest = split(g)
        v = v_ref[n]
        k = k_ref[n]
        q = q_ref[n]
        u = dot(jnp.concatenate([g_head, g_rest], axis=0), v, NT)
        u = u[0:8] + u[8:16]
        parts = []
        for j in range(GROUP):
            p = p_ref[n, L * j : L * (j + 1), :]
            pu = p * u[j : j + 1]
            parts.append((pu - p * jnp.sum(pu, axis=1, keepdims=True)) * (1.0 / math.sqrt(HD)))
        ds_head, ds_rest = split(jnp.concatenate(parts, axis=0))
        dq = dot(ds_head, k) + dot(ds_rest, k)
        dk = dot(ds_head, q, TN) + dot(ds_rest, q, TN)
        c_head, c_rest = split(csum_ref[n])
        dv = dot(
            jnp.concatenate([c_head, c_rest, c_head, c_rest], axis=0),
            jnp.concatenate([g_head, g_head, g_rest, g_rest], axis=0),
            TN,
        )
        dproj = jnp.concatenate(
            [unrope(dq[L * j : L * (j + 1)]) for j in range(GROUP)] + [unrope(dk), dv], axis=1
        )
        head_part, rest_part = split(ADAPTER_SCALE * dproj)
        low_grad = dot(up, head_part, NT) + dot(up, rest_part, NT)
        l_head, l_rest = split(low_grad)
        lanes = pl.ds(pl.multiple_of(n * L, L), L)
        dlow[0:LOW, lanes] = l_head
        dlow[LOW : 2 * LOW, lanes] = l_rest
        low = low_ref[n]
        dup[...] += dot(low, head_part, TN) + dot(low, rest_part, TN)

    sums[1, :, RING // 2 : RING] = jnp.zeros((N_FSDP, RING // 2, 8, HD), F32)
    for j in range(GROUP + 2):
        tile = GROUP * head + j if j < GROUP else (HQ + HK * (j - GROUP)) + head
        shard = tile // 3
        block = max(0, j - GROUP + 1)
        value = dup[ADAPTER_RANK * block : ADAPTER_RANK * (block + 1), HD * j : HD * (j + 1)]
        for i in range(2):
            sums[1, shard, RING // 2 + 2 * (tile % 3) + i] = value[8 * i : 8 * (i + 1)]
    for copy in copies:
        copy.wait()
    for f in range(N_FSDP):
        both = dot(dlow[...], tok[:, ROWS * f : ROWS * (f + 1)])
        value = both[0:LOW] + both[LOW : 2 * LOW]
        for b in range(ROWS // HD):
            for i in range(LOW // 8):
                group = b * (LOW // 8) + i
                sums[group // RING, f, group % RING] = value[8 * i : 8 * (i + 1), HD * b : HD * (b + 1)]
    keep_ref[...] = sums[core]
    give_ref[...] = sums[1 - core]


def backward(scalars, tokens, g_own, g_other, saved, cos, sin):
    n = len(tokens)
    return pl.pallas_call(
        backward_kernel,
        name="attention_backward",
        in_specs=[SMEM] + [ANY] * n + [VMEM] * 11,
        out_specs=[VMEM, VMEM],
        out_shape=[jax.ShapeDtypeStruct((N_FSDP, RING, 8, HD), F32)] * 2,
        scratch_shapes=[
            pltpu.VMEM((n * L, MODEL_WIDTH), BF16),
            pltpu.VMEM((2 * LOW, n * L), BF16),
            pltpu.VMEM((LOW, COLS), F32),
            pltpu.VMEM((n, 8, HD), F32),
            pltpu.VMEM((2, N_FSDP, RING, 8, HD), F32),
            pltpu.SemaphoreType.DMA((n,)),
        ],
        compiler_params=params(LARGE_VMEM),
        cost_estimate=cost(2 * n * L * MODEL_WIDTH * 2 * LOW, 15e6),
    )(scalars, *tokens, g_own, g_other, *saved, cos, sin)


def fold_kernel(parts_ref, out_ref):
    total = parts_ref[0]
    for n in range(1, N_FSDP):
        total = total + parts_ref[n]
    total = total.astype(BF16)
    for n in range(out_ref.shape[0]):
        out_ref[n] = total


def sum_kernel(parts_ref, out_ref):
    total = parts_ref[0].astype(F32)
    for n in range(1, parts_ref.shape[0]):
        total = total + parts_ref[n].astype(F32)
    out_ref[...] = total


def total_kernel(own_ref, other_ref, out_ref, squares_ref):
    total = own_ref[...] + other_ref[...]
    out_ref[...] = total
    squares = jnp.broadcast_to(jnp.sum(total * total, axis=0, keepdims=True), (8, HD))
    for n in range(N_FSDP):
        squares_ref[n] = squares


def finish_kernel(scalar_ref, own_ref, other_ref, squares_ref, squares_other_ref, down_ref, up_ref):
    core = scalar_ref[1]
    squares = jnp.sum(squares_ref[:, 0:1, :], axis=0) + jnp.sum(squares_other_ref[:, 0:1, :], axis=0)
    grad_norm = jnp.sqrt(jnp.sum(squares, axis=1, keepdims=True))
    unit_scale = math.sqrt(3 * MODEL_WIDTH * ADAPTER_RANK + (HQ + 2 * HK) * HD * ADAPTER_RANK)
    factor = jnp.minimum(1.0, MAX_NORM / (grad_norm + 1e-06)) * unit_scale

    def tile(group):
        half, spot = divmod(group, RING)
        a = own_ref[8 * spot : 8 * spot + 8, :]
        b = other_ref[8 * spot : 8 * spot + 8, :]
        return jnp.where(core == half, a, b) * factor

    for b in range(ROWS // HD):
        for i in range(LOW // 8):
            down_ref[8 * i : 8 * (i + 1), HD * b : HD * (b + 1)] = tile(b * (LOW // 8) + i)
    for b in range(UP_ROWS // HD):
        for i in range(ADAPTER_RANK // 8):
            group = (ROWS // HD) * (LOW // 8) + 2 * b + i
            up_ref[8 * i : 8 * (i + 1), HD * b : HD * (b + 1)] = tile(group)


def dp_pairs(move):
    pairs = []
    for d in range(N_DP):
        z, y, core = move(d // 4, (d // 2) % 2, d % 2)
        pairs.append((d, (z % (N_DP // 4)) * 4 + y * 2 + core))
    return pairs


Y_PARTNER = dp_pairs(lambda z, y, c: (z, 1 - y, c))
Z_GROUPS = [[4 * z + i for z in range(N_DP // 4)] for i in range(4)]
SIBLING = dp_pairs(lambda z, y, c: (z, y, 1 - c))
UPWARD = dp_pairs(lambda z, y, c: (z + 1, y, c))
DOWNWARD = dp_pairs(lambda z, y, c: (z - 1, y, c))
CORE_GROUPS = [[2 * i + c for i in range(RING)] for c in range(2)]


def to_sibling(x):
    return lax.ppermute(x, "dp", SIBLING)


def after(x, *others):
    return lax.optimization_barrier((x,) + others)[0]


def swap_dp(x):
    return lax.all_to_all(x, "dp", 0, 0, axis_index_groups=CORE_GROUPS)


def swap_z(x):
    return lax.all_to_all(x, "dp", 0, 0, axis_index_groups=Z_GROUPS)


def swap_fsdp(x):
    return lax.all_to_all(x, "fsdp", 0, 0)


def shards(
    query_rows, passage_rows, positive, layer_input, gain, frozen_weight, down_maps, up_maps
):
    dp = lax.axis_index("dp")
    core = dp % 2
    head = 2 * ((dp // 4) % 2) + core
    y_hi = (dp // 2) % 2
    cos, sin = (jnp.asarray(t) for t in rope_tables())

    scalars = jnp.stack([head, core, y_hi]).astype(jnp.int32)
    columns = [
        lax.dynamic_slice_in_dim(frozen_weight, GROUP * HD * head, GROUP * HD, 1),
        lax.dynamic_slice_in_dim(frozen_weight, HQ * HD + HD * head, HD, 1),
        lax.dynamic_slice_in_dim(frozen_weight, (HQ + HK) * HD + HD * head, HD, 1),
    ]
    maps = jnp.stack(
        [
            jnp.pad(down_maps.T[:MAP], ((0, 0), (0, COLS - ROWS))),
            jnp.concatenate(
                [
                    jnp.pad(down_maps.T[MAP:], ((0, 0), (0, COLS - ROWS))),
                    jnp.pad(up_maps.T, ((0, 0), (0, COLS - UP_ROWS))),
                ],
                axis=0,
            ),
        ]
    )
    mine = lax.dynamic_index_in_dim(maps, core, 0, keepdims=False)
    packed = jnp.concatenate([jnp.concatenate(columns, axis=1), mine], axis=0)
    weight = lax.all_gather(packed, "fsdp", axis=0)
    first, second = normalize(layer_input, gain)

    pair = jnp.stack([passage_rows, lax.ppermute(passage_rows, "dp", Y_PARTNER)])
    own = lax.all_to_all(
        jnp.broadcast_to(pair[None], (N_DP // 4, 2, 64, 256)), "dp", 0, 0, axis_index_groups=Z_GROUPS
    ).reshape(RING * 64, 256)
    own = after(own, first, second)
    other = to_sibling(own)
    from_below = lax.ppermute(after(first, own), "dp", UPWARD)
    from_above = lax.ppermute(after(second, own), "dp", DOWNWARD)

    partial = pl.pallas_call(
        partial_scores_kernel,
        name="partial_scores",
        out_shape=jax.ShapeDtypeStruct((N_FSDP, 72, 256), F32),
        compiler_params=params(),
        cost_estimate=cost(2 * 64 * 256 * 2048 * 2, 2e6),
    )(query_rows, own, other)
    scores = pl.pallas_call(
        finish_scores_kernel,
        name="finish_scores",
        out_shape=jax.ShapeDtypeStruct((N_FSDP, 72, 256), F32),
        compiler_params=params(),
        cost_estimate=cost(64 * 256 * 20, 1.2e6),
    )(swap_fsdp(partial))
    scores = after(swap_fsdp(scores), from_below, from_above)
    owner = positive // 64
    place = (
        jnp.where(owner % 2 == core, 0, RING * 64)
        + (owner // 4) * 128
        + jnp.where((owner // 2) % 2 == y_hi, 0, 64)
        + positive % 64
    ).astype(jnp.int32)
    query_grad, pulls, columns_sum, rerun = pl.pallas_call(
        query_grad_kernel,
        name="query_grad",
        out_shape=[
            jax.ShapeDtypeStruct((64, 256), F32),
            jax.ShapeDtypeStruct((N_FSDP, 64, 256), F32),
            jax.ShapeDtypeStruct((N_FSDP, 8, 256), F32),
            jax.ShapeDtypeStruct((N_FSDP, 2, 256), F32),
        ],
        compiler_params=params(),
        cost_estimate=cost(2 * 128 * 256 * 2048, 2e6),
    )(scores, query_rows, place.reshape(64, 1), own, other)
    g = swap_fsdp(rerun)

    keep, give = pl.pallas_call(
        passage_terms_kernel,
        name="passage_terms",
        out_shape=[jax.ShapeDtypeStruct((RING * 64, 256), F32)] * 2,
        compiler_params=params(),
        cost_estimate=cost(2 * 128 * 256 * 2048, 6e6),
    )(after(pulls, g), columns_sum, query_rows, own, other)
    received = to_sibling(give)

    tokens = [first, second, to_sibling(first), to_sibling(second)]
    tokens += [from_below, from_above, to_sibling(from_below), to_sibling(from_above)]
    sent = (keep + received).astype(BF16).reshape(N_DP // 4, 2, 64, 256)
    arrived = swap_z(sent)
    over_z = jnp.sum(arrived.astype(F32), axis=0)
    passage_grad = over_z[0] + lax.ppermute(over_z[1], "dp", Y_PARTNER)

    g = jnp.swapaxes(g, 0, 1)
    below, above = lax.ppermute(g[0:1], "dp", UPWARD), lax.ppermute(g[1:2], "dp", DOWNWARD)
    weight = after(weight, sent)
    maps_other = to_sibling(weight[:, ROWS:])
    *saved, = project(scalars, tokens, weight, maps_other, cos, sin)
    queries, keys = saved[:2]
    weights, sums = attend(queries, keys)
    below = after(below, queries)
    g_own = jnp.concatenate([g, below, above], axis=0)
    g_other = to_sibling(g_own)
    kept, given = backward(
        scalars, tokens, g_own, g_other, [queries, keys, saved[2], weights, sums, *saved[3:]], cos, sin
    )
    given = after(given, arrived)

    summed = kept + to_sibling(given)
    shared = pl.pallas_call(
        fold_kernel,
        name="fold_fsdp",
        out_shape=jax.ShapeDtypeStruct((N_DP // 4, RING * 8, HD), BF16),
        compiler_params=params(),
    )(swap_fsdp(summed.reshape(N_FSDP, RING * 8, HD)))
    half = pl.pallas_call(
        sum_kernel,
        name="sum_z",
        out_shape=jax.ShapeDtypeStruct((RING * 8, HD), F32),
        compiler_params=params(),
    )(swap_z(shared))
    total, squares = pl.pallas_call(
        total_kernel,
        name="total_dp",
        out_shape=[
            jax.ShapeDtypeStruct((RING * 8, HD), F32),
            jax.ShapeDtypeStruct((N_FSDP, 8, HD), F32),
        ],
        compiler_params=params(),
    )(half, lax.ppermute(half, "dp", Y_PARTNER))
    total_other = to_sibling(total)
    squares = swap_fsdp(squares)
    down, up = pl.pallas_call(
        finish_kernel,
        name="finish_clip",
        in_specs=[SMEM] + [VMEM] * 4,
        out_shape=[
            jax.ShapeDtypeStruct((LOW, ROWS), F32),
            jax.ShapeDtypeStruct((ADAPTER_RANK, UP_ROWS), F32),
        ],
        compiler_params=params(),
    )(scalars, total, total_other, squares, to_sibling(after(squares, passage_grad)))
    return query_grad, passage_grad, down.T, up.T


def solution(mesh):
    in_specs = (
        P("dp", "fsdp"),
        P("dp", "fsdp"),
        P("dp"),
        P(("dp", "fsdp"), None, None),
        P(),
        P("fsdp", None),
        P("fsdp", None),
        P("fsdp", None),
    )
    out_specs = (P("dp", "fsdp"), P("dp", "fsdp"), P("fsdp", None), P("fsdp", None))
    return jax.shard_map(shards, mesh=mesh, in_specs=in_specs, out_specs=out_specs, check_vma=False)
```
